32 devices in a mesh: group: 4 (over y, core), blk: 8 (over z, x).
Axes of the slice: x: 2, y: 2, z: 4, core: 2. Of those that a mesh axis runs over, the one named last changes fastest.
Arguments:
- points: bfloat16 [262144, 768], P(('group', 'blk')), may hold values from -128 to 128
- block_lists: int32 [2048, 4], P(('group', 'blk')), may hold values from 0 to 127, as said below
- centroids: bfloat16 [8192, 768], P('blk'), may hold values from -6 to 6
- dual_weights: bfloat16 [8192], P('blk'), may hold values from -1 to 1
Outputs:
- new_centroids: bfloat16 [8192, 768], P('blk')
- new_weights: bfloat16 [8192], P('blk')
The draws below stay inside these ranges and needn't reach their ends.
Inputs may be any that keep to these rules, and one draw needn't show every extreme that they name: `block_lists`: cycle position q (index q along blk) owns blocks q * 16 to (q + 1) * 16 - 1. For a tile held by a device at cycle position p, slot 0 names a block of position p - 1, slot 2 a block of position p + 1, and slots 1 and 3 two different blocks of position p, positions taken modulo the number of devices along blk.
All inputs are finite; a program needn't handle non-finite values.
Results may differ from the reference program's by a relative error of at most 0.0052.
Values may be sent and summed in bfloat16 or wider, within the bound.
No kernel may reach another device: no remote copies, remote signals or barrier semaphores. Data moves between devices by JAX's collectives and lax.ppermute only.
A program may use at most 128 MiB of HBM per device.

```python
import math
import jax
import jax.numpy as jnp
from jax import lax

D = 768
BLOCK = 64
TILE = 128
SLOTS = 4
ITERS = 2
CB_DEV = 16
P_DEV = 8192
K = 8192
POINTS = 262144


def drawn_lists(key):
    tile_count = POINTS // TILE
    cycle_size = K // (CB_DEV * BLOCK)
    tile_index = jnp.arange(tile_count, dtype=jnp.int32)
    position = tile_index // (P_DEV // TILE) % cycle_size
    keys = jax.random.split(jax.random.fold_in(key, 21), 4)
    lower = jax.random.randint(keys[0], (tile_count,), 0, CB_DEV, dtype=jnp.int32)
    upper = jax.random.randint(keys[1], (tile_count,), 0, CB_DEV, dtype=jnp.int32)
    own_first = jax.random.randint(keys[2], (tile_count,), 0, CB_DEV, dtype=jnp.int32)
    own_step = jax.random.randint(keys[3], (tile_count,), 1, CB_DEV, dtype=jnp.int32)
    left_block = (position - 1) % cycle_size * CB_DEV + lower
    right_block = (position + 1) % cycle_size * CB_DEV + upper
    own_one = position * CB_DEV + own_first
    own_two = position * CB_DEV + (own_first + own_step) % CB_DEV
    return jnp.stack([left_block, own_one, right_block, own_two], axis=-1).astype(jnp.int32)


def drawn_centroids(key):
    values = jnp.clip(jax.random.normal(jax.random.fold_in(key, 22), (K, D), jnp.float32), -6.0, 6.0)
    return values.astype(jnp.bfloat16).astype(jnp.float32)


def drawn_weights(key):
    values = jax.random.uniform(jax.random.fold_in(key, 23), (K,), jnp.float32, -1.0, 1.0)
    return values.astype(jnp.bfloat16).astype(jnp.float32)


def draw_block_lists(key, part):
    return drawn_lists(key).astype(jnp.int32)


def draw_centroids(key, part):
    return drawn_centroids(key).astype(jnp.bfloat16)


def draw_dual_weights(key, part):
    return drawn_weights(key).astype(jnp.bfloat16)


def draw_points(key, part):
    keys = jax.random.split(jax.random.fold_in(key, 24), 1)
    values = jnp.clip(jax.random.normal(keys[0], (POINTS, D), jnp.float32), -6.0, 6.0)
    values = jnp.clip(values, -128.0, 128.0)
    return values.astype(jnp.bfloat16)


def setup_inputs(seed: int = 0) -> dict:
    splits = jax.random.split(jax.random.key(seed), 5)
    return {
        "points": draw_points(jax.random.fold_in(splits[4], 71), 0),
        "block_lists": draw_block_lists(jax.random.fold_in(splits[4], 71), 0),
        "centroids": draw_centroids(jax.random.fold_in(splits[4], 71), 0),
        "dual_weights": draw_dual_weights(jax.random.fold_in(splits[4], 71), 0),
    }


prior_mass = 1.0
dual_step = 0.5


def assign_pass(points, block_lists, centroids, weights):
    block_count = K // BLOCK
    base = centroids.astype(jnp.float32)
    offsets = weights.astype(jnp.float32) - jnp.sum(base * base, axis=1) * (16.0 / D)
    cand_blocks = base.reshape(block_count, BLOCK, D)
    offset_blocks = offsets.reshape(block_count, BLOCK)
    tile_count = block_lists.shape[0]
    group_size = math.gcd(tile_count, 64)
    tiled_points = points.reshape(tile_count // group_size, group_size, TILE, D)
    tiled_ids = block_lists.reshape(tile_count // group_size, group_size, SLOTS)

    def tile_step(running, packet):
        sum_num, sum_mass = running
        tile_points, block_ids = packet
        point_vals = tile_points.astype(jnp.float32)
        candidates = cand_blocks[block_ids].reshape(group_size, SLOTS * BLOCK, D)
        scores = jnp.einsum("tpd,tkd->tpk", point_vals, candidates) * (32.0 / D)
        scores = scores + offset_blocks[block_ids].reshape(group_size, 1, SLOTS * BLOCK)
        membership = lax.optimization_barrier(jax.nn.softmax(scores, axis=-1).astype(jnp.bfloat16)).astype(jnp.float32)
        masses = jnp.sum(membership, axis=1).reshape(group_size * SLOTS, BLOCK)
        numerator = jnp.einsum("tpk,tpd->tkd", membership, point_vals).reshape(group_size * SLOTS, BLOCK, D)
        flat_ids = block_ids.reshape(-1)
        return (sum_num.at[flat_ids].add(numerator), sum_mass.at[flat_ids].add(masses)), None

    start = (jnp.zeros((block_count, BLOCK, D), jnp.float32), jnp.zeros((block_count, BLOCK), jnp.float32))
    (sum_num, sum_mass), _ = lax.scan(tile_step, start, (tiled_points, tiled_ids))
    return sum_num.reshape(K, D), sum_mass.reshape(K)


def reference(points, block_lists, centroids, dual_weights):
    target = POINTS / K
    weights = dual_weights
    for sweep in range(ITERS):
        totals_num, totals_mass = assign_pass(points, block_lists, centroids, weights)
        base = centroids.astype(jnp.float32)
        centroids = ((totals_num + prior_mass * base) / (totals_mass + prior_mass)[:, None]).astype(jnp.bfloat16)
        weights = (weights.astype(jnp.float32) + dual_step * (1.0 - totals_mass / target)).astype(jnp.bfloat16)
    return centroids, weights
```

```python
import functools

import jax
import jax.numpy as jnp
from jax import lax
from jax.experimental import pallas as pl
from jax.experimental.pallas import tpu as pltpu
from jax.sharding import PartitionSpec as P

BLOCK = 64
TILE = 128
SLOTS = 4
ITERS = 2
TAIL = 16
STEP_TILES = 4
prior_mass = 1.0
dual_step = 0.5
F32 = jnp.float32
BF16 = jnp.bfloat16
VMEM_LIMIT = 56 * 1024 * 1024


def swap(x, bit):
    groups = lax.axis_size("group")
    return lax.ppermute(x, "group", [(i, i ^ bit) for i in range(groups)])


def core_swap(x):
    return swap(x, 1)


def plane_swap(x):
    return swap(x, 2)


def along(x, distance):
    count = lax.axis_size("blk")
    return lax.ppermute(x, "blk", [((i - distance) % count, i) for i in range(count)])


def eye():
    shape = (TILE, TILE)
    return lax.broadcasted_iota(jnp.int32, shape, 0) == lax.broadcasted_iota(jnp.int32, shape, 1)


def to_column(row):
    return jnp.sum(jnp.where(eye(), row, 0.0), axis=1, keepdims=True)


def to_row(column):
    return jnp.sum(jnp.where(eye(), column, 0.0), axis=0, keepdims=True)


def split_masses(row):
    high = row.astype(BF16)
    rest = row - high.astype(F32)
    mid = rest.astype(BF16)
    low = (rest - mid.astype(F32)).astype(BF16)
    return jnp.concatenate([high, mid, low], axis=1)


def tail_of(row):
    wide = jnp.broadcast_to(row.astype(F32), (TAIL, row.shape[1]))
    first = lax.broadcasted_iota(jnp.int32, wide.shape, 0) == 0
    return jnp.where(first, wide, 0.0)


def mass_of(tail, quarter):
    row = tail[0:1, :].astype(F32)
    return row[:, :quarter] + row[:, quarter : 2 * quarter] + row[:, 2 * quarter : 3 * quarter]


def tiles_kernel(rows, ids_ref, me_ref, points_ref, *refs):
    quarter = rows // 4
    packet = quarter + TAIL
    half = rows // 2
    packets = refs[:12]
    sends = refs[12:15]
    keeps = refs[15:18]
    near, tails, offs, acc, macc, stage, ktail, in_sem, out_sem = refs[18:]
    step = pl.program_id(0)
    core = me_ref[0]
    plane = me_ref[1]

    def place(side, j):
        c = core if j < 2 else 1 - core
        y = plane if j % 2 == 0 else 1 - plane
        return side * 4 + c * 2 + y

    def arrivals():
        out = []
        for side in range(3):
            for j in range(4):
                n = side * 4 + j
                at = place(side, j)
                out.append(
                    pltpu.make_async_copy(
                        packets[n].at[pl.ds(0, quarter)],
                        near.at[pl.ds(pl.multiple_of(at * quarter, quarter), quarter)],
                        in_sem.at[2 * n],
                    )
                )
                out.append(
                    pltpu.make_async_copy(
                        packets[n].at[pl.ds(quarter, TAIL)],
                        tails.at[pl.ds(pl.multiple_of(at * TAIL, TAIL), TAIL)],
                        in_sem.at[2 * n + 1],
                    )
                )
        return out

    @pl.when(step == 0)
    def _():
        copies = arrivals()
        for copy in copies:
            copy.start()

        @pl.loop(0, 3 * rows // BLOCK)
        def _(b):
            at = pl.ds(pl.multiple_of(b * BLOCK, BLOCK), BLOCK)
            acc[at, :] = jnp.zeros((BLOCK, acc.shape[1]), F32)
            macc[at, :] = jnp.zeros((BLOCK, TILE), F32)

        for copy in copies:
            copy.wait()

        width = near.shape[1]

        @pl.loop(0, 12)
        def _(n):
            tail = tails[pl.ds(pl.multiple_of(n * TAIL, TAIL), TAIL), :].astype(F32)
            for k in range(quarter // TILE):
                at = pl.ds(pl.multiple_of(n * quarter + k * TILE, TILE), TILE)
                base = near[at, :].astype(F32)
                squares = jnp.sum(base * base, axis=1, keepdims=True)
                weights = to_column(tail[0:1, k * TILE : (k + 1) * TILE])
                offs[at, :] = jnp.broadcast_to(weights - squares * (16.0 / width), (TILE, TILE))

    width = near.shape[1]
    for t in range(STEP_TILES):
        points = points_ref[pl.ds(t * TILE, TILE), :]
        tile = step * STEP_TILES + t
        at = [
            pl.ds(pl.multiple_of(ids_ref[tile * SLOTS + k] * BLOCK, BLOCK), BLOCK)
            for k in range(SLOTS)
        ]
        cand = jnp.concatenate([near[a, :] for a in at], axis=0)
        off = jnp.concatenate([offs[a, :] for a in at], axis=0)
        scores = lax.dot_general(
            cand, points, (((1,), (1,)), ((), ())), preferred_element_type=F32
        )
        scores = scores * (32.0 / width) + off
        top = jnp.max(scores, axis=0, keepdims=True)
        raw = jnp.exp(scores - top)
        total = jnp.sum(raw, axis=0, keepdims=True)
        member = (raw * (1.0 / total)).astype(BF16)
        numerator = jnp.dot(member, points, preferred_element_type=F32)
        masses = member.astype(F32)
        for k in range(SLOTS):
            acc[at[k], :] += numerator[k * BLOCK : (k + 1) * BLOCK]
            macc[at[k], :] += masses[k * BLOCK : (k + 1) * BLOCK]

    @pl.when(step == pl.num_programs(0) - 1)
    def _():
        copies = []
        for side in (0, 2, 1):
            for y in range(2):
                n = side * 2 + y
                mine = pl.multiple_of(side * rows + core * half + y * quarter, quarter)
                other = pl.multiple_of(side * rows + (1 - core) * half + y * quarter, quarter)

                def masses_at(start):
                    return jnp.concatenate(
                        [
                            to_row(
                                jnp.sum(
                                    macc[pl.ds(start + k * TILE, TILE), :], axis=1, keepdims=True
                                )
                            )
                            for k in range(quarter // TILE)
                        ],
                        axis=1,
                    )

                stage[side, pl.ds(y * packet, quarter), :] = acc[pl.ds(other, quarter), :].astype(
                    BF16
                )
                stage[side, pl.ds(y * packet + quarter, TAIL), :] = tail_of(
                    split_masses(masses_at(other))
                ).astype(BF16)
                row = masses_at(mine)
                ktail[n] = tail_of(jnp.concatenate([row, row * 0.0, row * 0.0], axis=1))
                copies.append(
                    pltpu.make_async_copy(
                        acc.at[pl.ds(mine, quarter)],
                        keeps[side].at[pl.ds(y * packet, quarter)],
                        out_sem.at[n],
                    )
                )
                copies[-1].start()
                copies.append(
                    pltpu.make_async_copy(
                        ktail.at[n],
                        keeps[side].at[pl.ds(y * packet + quarter, TAIL)],
                        out_sem.at[6 + n],
                    )
                )
                copies[-1].start()
            copies.append(
                pltpu.make_async_copy(stage.at[side], sends[side], out_sem.at[12 + side])
            )
            copies[-1].start()
        for copy in copies:
            copy.wait()


def assign_tiles(points, ids, me, packets, rows):
    count, width = points.shape
    quarter = rows // 4
    packet = quarter + TAIL
    tiles = count // TILE
    any_spec = pl.BlockSpec(memory_space=pl.ANY)
    step_rows = STEP_TILES * TILE
    outs = pl.pallas_call(
        functools.partial(tiles_kernel, rows),
        grid_spec=pltpu.PrefetchScalarGridSpec(
            num_scalar_prefetch=2,
            grid=(tiles // STEP_TILES,),
            in_specs=[pl.BlockSpec((step_rows, width), lambda i, ids, me: (i, 0))]
            + [any_spec] * 12,
            out_specs=[any_spec] * 6,
            scratch_shapes=[
                pltpu.VMEM((3 * rows, width), BF16),
                pltpu.VMEM((12 * TAIL, width), BF16),
                pltpu.VMEM((3 * rows, TILE), F32),
                pltpu.VMEM((3 * rows, width), F32),
                pltpu.VMEM((3 * rows, TILE), F32),
                pltpu.VMEM((3, 2 * packet, width), BF16),
                pltpu.VMEM((6, TAIL, width), F32),
                pltpu.SemaphoreType.DMA((24,)),
                pltpu.SemaphoreType.DMA((15,)),
            ],
        ),
        out_shape=[jax.ShapeDtypeStruct((2 * packet, width), BF16)] * 3
        + [jax.ShapeDtypeStruct((2 * packet, width), F32)] * 3,
        compiler_params=pltpu.CompilerParams(vmem_limit_bytes=VMEM_LIMIT),
        cost_estimate=pl.CostEstimate(
            flops=4 * count * SLOTS * BLOCK * width,
            bytes_accessed=2 * count * width,
            transcendentals=count * SLOTS * BLOCK,
        ),
        name="tiles",
    )(ids, me, points, *packets)
    return outs[:3], outs[3:]


def sum_kernel(quarter, me_ref, *refs):
    out = refs[-1]
    terms = refs[:-1]
    total = terms[0][pl.ds(0, quarter), :].astype(F32)
    for term in terms[1:]:
        total = total + term[pl.ds(0, quarter), :].astype(F32)
    out[pl.ds(0, quarter), :] = total.astype(BF16)
    mass = mass_of(terms[0][pl.ds(quarter, TAIL), :], quarter)
    for term in terms[1:]:
        mass = mass + mass_of(term[pl.ds(quarter, TAIL), :], quarter)
    out[pl.ds(quarter, TAIL), :] = tail_of(split_masses(mass)).astype(BF16)


def part_spec(packet, width, other):
    if other is None:
        return pl.BlockSpec((packet, width), lambda i, me: (0, 0))
    if other:
        return pl.BlockSpec((packet, width), lambda i, me: (1 - me[1], 0))
    return pl.BlockSpec((packet, width), lambda i, me: (me[1], 0))


def add_packets(me, pairs, singles, other):
    width = pairs[0].shape[1]
    packet = pairs[0].shape[0] // 2
    terms = list(pairs) + list(singles)
    return pl.pallas_call(
        functools.partial(sum_kernel, packet - TAIL),
        grid_spec=pltpu.PrefetchScalarGridSpec(
            num_scalar_prefetch=1,
            grid=(1,),
            in_specs=[part_spec(packet, width, other)] * len(pairs)
            + [part_spec(packet, width, None)] * len(singles),
            out_specs=part_spec(packet, width, None),
        ),
        out_shape=jax.ShapeDtypeStruct((packet, width), BF16),
        compiler_params=pltpu.CompilerParams(vmem_limit_bytes=VMEM_LIMIT),
        cost_estimate=pl.CostEstimate(
            flops=packet * width * len(terms),
            bytes_accessed=sum(t.size * t.dtype.itemsize for t in terms),
            transcendentals=0,
        ),
        name="add_packets",
    )(me, *terms)


def renew_kernel(quarter, target, me_ref, base_ref, *refs):
    out = refs[-1]
    terms = refs[:-1]
    mass = mass_of(terms[0][pl.ds(quarter, TAIL), :], quarter)
    for term in terms[1:]:
        mass = mass + mass_of(term[pl.ds(quarter, TAIL), :], quarter)
    weights = base_ref[pl.ds(quarter, TAIL), :].astype(F32)[0:1, :quarter]
    renewed = weights + dual_step * (1.0 - mass / target)
    zero = renewed * 0.0
    out[pl.ds(quarter, TAIL), :] = tail_of(
        jnp.concatenate([renewed, zero, zero], axis=1)
    ).astype(BF16)
    for k in range(quarter // TILE):
        at = pl.ds(k * TILE, TILE)
        total = terms[0][at, :].astype(F32)
        for term in terms[1:]:
            total = total + term[at, :].astype(F32)
        base = base_ref[at, :].astype(F32)
        column = to_column(mass[:, k * TILE : (k + 1) * TILE]) + prior_mass
        out[at, :] = ((total + prior_mass * base) / column).astype(BF16)


def renew(me, base, pairs, singles, target):
    width = pairs[0].shape[1]
    packet = pairs[0].shape[0] // 2
    terms = list(pairs) + list(singles)
    return pl.pallas_call(
        functools.partial(renew_kernel, packet - TAIL, target),
        grid_spec=pltpu.PrefetchScalarGridSpec(
            num_scalar_prefetch=1,
            grid=(1,),
            in_specs=[part_spec(packet, width, None)]
            + [part_spec(packet, width, False)] * len(pairs)
            + [part_spec(packet, width, None)] * len(singles),
            out_specs=part_spec(packet, width, None),
        ),
        out_shape=jax.ShapeDtypeStruct((packet, width), BF16),
        compiler_params=pltpu.CompilerParams(vmem_limit_bytes=VMEM_LIMIT),
        name="renew",
    )(me, base, *terms)


def per_device(points, block_lists, centroids, dual_weights):
    rows, width = centroids.shape
    quarter = rows // 4
    own_blocks = rows // BLOCK
    cycle_size = lax.axis_size("blk")
    position = lax.axis_index("blk")
    groups = lax.axis_size("group")
    member = lax.axis_index("group")
    core, plane = member % 2, member // 2
    me = jnp.stack([core, plane]).astype(jnp.int32)
    target = points.shape[0] * groups / rows
    owner = block_lists // own_blocks
    near_ids = (owner - position + 1) % cycle_size * own_blocks + block_lists % own_blocks
    near_ids = near_ids.reshape(-1).astype(jnp.int32)

    def start_packet(c, y):
        first = (c * 2 + y) * quarter
        block = lax.dynamic_slice_in_dim(centroids, first, quarter, 0)
        row = lax.dynamic_slice_in_dim(dual_weights, first, quarter, 0)
        tail = jnp.pad(row[None, :], ((0, TAIL - 1), (0, width - quarter)))
        return jnp.concatenate([block, tail], axis=0)

    def spread(packet):
        beside = plane_swap(packet)
        return [packet, beside, core_swap(packet), core_swap(beside)]

    mine = start_packet(core, plane)
    own = None
    for sweep in range(ITERS):
        lower, upper = along(mine, 1), along(mine, -1)
        if sweep == 0:
            own = [
                mine,
                start_packet(core, 1 - plane),
                start_packet(1 - core, plane),
                start_packet(1 - core, 1 - plane),
            ]
        else:
            own = spread(mine)
        packets = spread(lower) + own + spread(upper)
        sends, keeps = assign_tiles(points, near_ids, me, packets, rows)
        halves = [None] * 3
        for side in (0, 2, 1):
            halves[side] = (keeps[side], core_swap(sends[side]))
        planes = [None] * 3
        for side in (0, 2, 1):
            planes[side] = plane_swap(add_packets(me, halves[side], [], True))
        down = along(add_packets(me, halves[0], [planes[0]], False), -1)
        up = along(add_packets(me, halves[2], [planes[2]], False), 1)
        mine = renew(me, mine, halves[1], [planes[1], down, up], target)
    own = spread(mine)
    order = jnp.stack(
        [core * 2 + plane, core * 2 + 1 - plane, 2 - core * 2 + plane, 3 - core * 2 - plane]
    )
    stacked = jnp.stack(own)[jnp.argsort(order)]
    new_centroids = stacked[:, :quarter, :].reshape(rows, width)
    new_weights = stacked[:, quarter, :quarter].reshape(rows)
    return (new_centroids, new_weights)


def solution(mesh):
    return jax.shard_map(
        per_device,
        mesh=mesh,
        in_specs=(P(("group", "blk"), None), P(("group", "blk"), None), P("blk", None), P("blk")),
        out_specs=(P("blk", None), P("blk")),
        check_vma=False,
    )
```

```python
import functools

import jax
import jax.numpy as jnp
from jax import lax
from jax.experimental import pallas as pl
from jax.experimental.pallas import tpu as pltpu
from jax.sharding import PartitionSpec as P

BLOCK = 64
TILE = 128
SLOTS = 4
ITERS = 2
TAIL = 16
STEP_TILES = 8
CHUNKS = 2
prior_mass = 1.0
dual_step = 0.5
F32 = jnp.float32
BF16 = jnp.bfloat16
VMEM_LIMIT = 36 * 1024 * 1024
SMALL_LIMIT = 16 * 1024 * 1024


def swap(x, bit):
    groups = lax.axis_size("group")
    return lax.ppermute(x, "group", [(i, i ^ bit) for i in range(groups)])


def core_swap(x):
    return swap(x, 1)


def plane_swap(x):
    return swap(x, 2)


def pair_swap(x):
    count = lax.axis_size("blk")
    return lax.ppermute(x, "blk", [(i, i ^ 1) for i in range(count)])


def outward(x):
    count = lax.axis_size("blk")
    return lax.ppermute(x, "blk", [(i, (i + 2 - i % 2 * 4) % count) for i in range(count)])


def inward(x):
    count = lax.axis_size("blk")
    return lax.ppermute(x, "blk", [((i + 2 - i % 2 * 4) % count, i) for i in range(count)])


def ranges(quarter):
    size = quarter // CHUNKS
    return [(k * size, (k + 1) * size) for k in range(CHUNKS)]


def part_rows(part, quarter):
    return part[1] - part[0] + (TAIL if part[1] == quarter else 0)


def eye():
    shape = (TILE, TILE)
    return lax.broadcasted_iota(jnp.int32, shape, 0) == lax.broadcasted_iota(jnp.int32, shape, 1)


def to_column(row):
    return jnp.sum(jnp.where(eye(), row, 0.0), axis=1, keepdims=True)


def to_row(column):
    return jnp.sum(jnp.where(eye(), column, 0.0), axis=0, keepdims=True)


def split_masses(row):
    high = row.astype(BF16)
    rest = row - high.astype(F32)
    mid = rest.astype(BF16)
    low = (rest - mid.astype(F32)).astype(BF16)
    return jnp.concatenate([high, mid, low], axis=1)


def tail_of(row):
    wide = jnp.broadcast_to(row.astype(F32), (TAIL, row.shape[1]))
    first = lax.broadcasted_iota(jnp.int32, wide.shape, 0) == 0
    return jnp.where(first, wide, 0.0)


def mass_of(tail, quarter):
    row = tail[0:1, :].astype(F32)
    return row[:, :quarter] + row[:, quarter : 2 * quarter] + row[:, 2 * quarter : 3 * quarter]


def tiles_kernel(rows, sizes, ids_ref, me_ref, points_ref, *refs):
    quarter = rows // 4
    packet = quarter + TAIL
    half = rows // 2
    count = sum(len(parts) for side in sizes for parts in side)
    parts_refs = list(refs[:count])
    sends = refs[count : count + 3]
    keeps = refs[count + 3 : count + 6]
    near, tails, offs, acc, macc, in_sem = refs[count + 6 :]
    step = pl.program_id(0)
    core = me_ref[0]
    plane = me_ref[1]

    def arrivals():
        out = []
        left = list(parts_refs)
        for side in range(3):
            for j in range(4):
                c = core if j < 2 else 1 - core
                y = plane if j % 2 == 0 else 1 - plane
                at = side * 4 + c * 2 + y
                first = 0
                for size in sizes[side][j]:
                    ref = left.pop(0)
                    last = min(first + size, quarter)
                    out.append(
                        pltpu.make_async_copy(
                            ref.at[pl.ds(0, last - first)],
                            near.at[
                                pl.ds(pl.multiple_of(at * quarter + first, TILE), last - first)
                            ],
                            in_sem.at[len(out)],
                        )
                    )
                    if first + size > quarter:
                        out.append(
                            pltpu.make_async_copy(
                                ref.at[pl.ds(last - first, TAIL)],
                                tails.at[pl.ds(pl.multiple_of(at * TAIL, TAIL), TAIL)],
                                in_sem.at[len(out)],
                            )
                        )
                    first = last
        return out

    width = near.shape[1]

    @pl.when(step == 0)
    def _():
        copies = arrivals()
        for copy in copies:
            copy.start()

        @pl.loop(0, 3 * rows // BLOCK)
        def _(b):
            at = pl.ds(pl.multiple_of(b * BLOCK, BLOCK), BLOCK)
            acc[at, :] = jnp.zeros((BLOCK, width), F32)
            macc[at, :] = jnp.zeros((BLOCK, TILE), F32)

        for copy in copies:
            copy.wait()

        @pl.loop(0, 12)
        def _(n):
            tail = tails[pl.ds(pl.multiple_of(n * TAIL, TAIL), TAIL), :].astype(F32)
            for k in range(quarter // TILE):
                at = pl.ds(pl.multiple_of(n * quarter + k * TILE, TILE), TILE)
                base = near[at, :].astype(F32)
                squares = jnp.sum(base * base, axis=1, keepdims=True)
                weights = to_column(tail[0:1, k * TILE : (k + 1) * TILE])
                offs[at, :] = jnp.broadcast_to(weights - squares * (16.0 / width), (TILE, TILE))

    def blocks_of(t):
        tile = step * STEP_TILES + t
        return [
            pl.ds(pl.multiple_of(ids_ref[tile * SLOTS + k] * BLOCK, BLOCK), BLOCK)
            for k in range(SLOTS)
        ]

    members = []
    for t in range(STEP_TILES):
        points = points_ref[pl.ds(t * TILE, TILE), :]
        at = blocks_of(t)
        cand = jnp.concatenate([near[a, :] for a in at], axis=0)
        off = jnp.concatenate([offs[a, :] for a in at], axis=0)
        scores = lax.dot_general(
            cand, points, (((1,), (1,)), ((), ())), preferred_element_type=F32
        )
        scores = scores * (32.0 / width) + off
        top = jnp.max(scores, axis=0, keepdims=True)
        raw = jnp.exp(scores - top)
        total = jnp.sum(raw, axis=0, keepdims=True)
        members.append((raw * (1.0 / total)).astype(BF16))
    for t in range(STEP_TILES):
        points = points_ref[pl.ds(t * TILE, TILE), :]
        at = blocks_of(t)
        numerator = jnp.dot(members[t], points, preferred_element_type=F32)
        masses = members[t].astype(F32)
        for k in range(SLOTS):
            acc[at[k], :] += numerator[k * BLOCK : (k + 1) * BLOCK]
            macc[at[k], :] += masses[k * BLOCK : (k + 1) * BLOCK]

    @pl.when(step == pl.num_programs(0) - 1)
    def _():
        def masses_at(start):
            return jnp.concatenate(
                [
                    to_row(jnp.sum(macc[pl.ds(start + k * TILE, TILE), :], axis=1, keepdims=True))
                    for k in range(quarter // TILE)
                ],
                axis=1,
            )

        for side in range(3):
            for y in range(2):
                mine = pl.multiple_of(side * rows + core * half + y * quarter, quarter)
                other = pl.multiple_of(side * rows + (1 - core) * half + y * quarter, quarter)
                body = pl.ds(y * packet, quarter)
                tail = pl.ds(y * packet + quarter, TAIL)
                sends[side][body, :] = acc[pl.ds(other, quarter), :].astype(BF16)
                sends[side][tail, :] = tail_of(split_masses(masses_at(other))).astype(BF16)
                row = masses_at(mine)
                keeps[side][body, :] = acc[pl.ds(mine, quarter), :]
                keeps[side][tail, :] = tail_of(
                    jnp.concatenate([row, row * 0.0, row * 0.0], axis=1)
                )


def assign_tiles(points, ids, me, packets, rows):
    count, width = points.shape
    quarter = rows // 4
    packet = quarter + TAIL
    tiles = count // TILE
    any_spec = pl.BlockSpec(memory_space=pl.ANY)
    vmem_spec = pl.BlockSpec(memory_space=pltpu.VMEM)
    step_rows = STEP_TILES * TILE
    sizes = [[[part.shape[0] for part in parts] for parts in side] for side in packets]
    arrays = [part for side in packets for parts in side for part in parts]
    outs = pl.pallas_call(
        functools.partial(tiles_kernel, rows, sizes),
        grid_spec=pltpu.PrefetchScalarGridSpec(
            num_scalar_prefetch=2,
            grid=(tiles // STEP_TILES,),
            in_specs=[pl.BlockSpec((step_rows, width), lambda i, ids, me: (i, 0))]
            + [any_spec] * len(arrays),
            out_specs=[vmem_spec] * 6,
            scratch_shapes=[
                pltpu.VMEM((3 * rows, width), BF16),
                pltpu.VMEM((12 * TAIL, width), BF16),
                pltpu.VMEM((3 * rows, TILE), F32),
                pltpu.VMEM((3 * rows, width), F32),
                pltpu.VMEM((3 * rows, TILE), F32),
                pltpu.SemaphoreType.DMA((len(arrays) + 12,)),
            ],
        ),
        out_shape=[jax.ShapeDtypeStruct((2 * packet, width), BF16)] * 3
        + [jax.ShapeDtypeStruct((2 * packet, width), F32)] * 3,
        compiler_params=pltpu.CompilerParams(vmem_limit_bytes=VMEM_LIMIT),
        cost_estimate=pl.CostEstimate(
            flops=4 * count * SLOTS * BLOCK * width,
            bytes_accessed=2 * count * width,
            transcendentals=count * SLOTS * BLOCK,
        ),
        name="tiles",
    )(ids, me, points, *arrays)
    return outs[:3], outs[3:]


def small_call(kernel, me, arrays, outs, name):
    vmem_spec = pl.BlockSpec(memory_space=pltpu.VMEM)
    return pl.pallas_call(
        kernel,
        in_specs=[pl.BlockSpec(memory_space=pltpu.SMEM)] + [vmem_spec] * len(arrays),
        out_specs=[vmem_spec] * len(outs),
        out_shape=outs,
        compiler_params=pltpu.CompilerParams(vmem_limit_bytes=SMALL_LIMIT),
        cost_estimate=pl.CostEstimate(
            flops=sum(a.size for a in arrays),
            bytes_accessed=sum(a.size * a.dtype.itemsize for a in arrays),
            transcendentals=0,
        ),
        name=name,
    )(me, *arrays)


def sum_kernel(quarter, pairs, other, parts, me_ref, *refs):
    terms = refs[: len(refs) - len(parts)]
    outs = refs[len(refs) - len(parts) :]
    plane = 1 - me_ref[1] if other else me_ref[1]
    start = plane * (quarter + TAIL)

    def rows_of(first, size):
        at = [pl.ds(pl.multiple_of(start + first, TAIL), size)] * pairs
        at += [pl.ds(first - parts[0][0], size)] * (len(terms) - pairs)
        return [term[a, :] for term, a in zip(terms, at)]

    for (first, last), out in zip(parts, outs):
        size = last - first
        out[pl.ds(0, size), :] = sum(r.astype(F32) for r in rows_of(first, size)).astype(BF16)
        if last == quarter:
            mass = sum(mass_of(r, quarter) for r in rows_of(quarter, TAIL))
            out[pl.ds(size, TAIL), :] = tail_of(split_masses(mass)).astype(BF16)


def add_packets(me, pairs, singles, other, parts):
    packet, width = pairs[0].shape[0] // 2, pairs[0].shape[1]
    quarter = packet - TAIL
    return small_call(
        functools.partial(sum_kernel, quarter, len(pairs), other, parts),
        me,
        [*pairs, *singles],
        [jax.ShapeDtypeStruct((part_rows(p, quarter), width), BF16) for p in parts],
        "add_packets",
    )


def renew_kernel(quarter, target, whole, parts, me_ref, base, keep, beside, plane_sum, *refs):
    arrived = refs[: len(parts)]
    outs = refs[len(parts) :]
    start = me_ref[1] * (quarter + TAIL)
    mass = mass_of(arrived[-1][pl.ds(parts[-1][1] - parts[-1][0], TAIL), :], quarter)
    mass = mass + mass_of(plane_sum[pl.ds(quarter, TAIL), :], quarter)
    for term in (keep, beside):
        tail = term[pl.ds(pl.multiple_of(start + quarter, TAIL), TAIL), :]
        mass = mass + mass_of(tail, quarter)
    weights = base[pl.ds(quarter, TAIL), :].astype(F32)[0:1, :quarter]
    renewed = weights + dual_step * (1.0 - mass / target)
    zero = renewed * 0.0
    tail = tail_of(jnp.concatenate([renewed, zero, zero], axis=1)).astype(BF16)
    for k, (first, last) in enumerate(parts):
        for row in range(first, last, TILE):
            here = pl.ds(pl.multiple_of(start + row, TAIL), TILE)
            total = keep[here, :] + beside[here, :].astype(F32)
            total = total + plane_sum[pl.ds(row, TILE), :].astype(F32)
            total = total + arrived[k][pl.ds(row - first, TILE), :].astype(F32)
            column = to_column(mass[:, row : row + TILE]) + prior_mass
            total = total + prior_mass * base[pl.ds(row, TILE), :].astype(F32)
            fresh = (total / column).astype(BF16)
            outs[k][pl.ds(row - first, TILE), :] = fresh
            if whole:
                outs[-1][pl.ds(row, TILE), :] = fresh
    outs[len(parts) - 1][pl.ds(parts[-1][1] - parts[-1][0], TAIL), :] = tail
    if whole:
        outs[-1][pl.ds(quarter, TAIL), :] = tail


def renew(me, base, keep, beside, plane_sum, arrived, target, whole):
    packet, width = base.shape
    quarter = packet - TAIL
    parts = ranges(quarter)
    outs = [jax.ShapeDtypeStruct((part_rows(p, quarter), width), BF16) for p in parts]
    if whole:
        outs.append(jax.ShapeDtypeStruct((packet, width), BF16))
    return small_call(
        functools.partial(renew_kernel, quarter, target, whole, parts),
        me,
        [base, keep, beside, plane_sum, *arrived],
        outs,
        "renew",
    )


def finish_kernel(rows, parts, me_ref, *refs):
    quarter = rows // 4
    n = 4 * len(parts)
    packets = refs[:n]
    out, weights_out, tails, sem = refs[n:]
    core, plane = me_ref[0], me_ref[1]
    copies = []
    places = []
    for j in range(4):
        c = core if j < 2 else 1 - core
        y = plane if j % 2 == 0 else 1 - plane
        places.append(c * 2 + y)
        for k, (first, last) in enumerate(parts):
            ref = packets[j * len(parts) + k]
            at = pl.multiple_of(places[j] * quarter + first, TILE)
            copies.append(
                pltpu.make_async_copy(
                    ref.at[pl.ds(0, last - first)],
                    out.at[pl.ds(at, last - first)],
                    sem.at[len(copies)],
                )
            )
            if last == quarter:
                copies.append(
                    pltpu.make_async_copy(
                        ref.at[pl.ds(last - first, TAIL)], tails.at[j], sem.at[len(copies)]
                    )
                )
    for copy in copies:
        copy.start()
    for copy in copies:
        copy.wait()
    found = [tails[j][0:1, :quarter].astype(F32) for j in range(4)]
    lines = []
    for q in range(4):
        line = found[0]
        for j in range(1, 4):
            line = jnp.where(places[j] == q, found[j], line)
        lines.append(line)
    weights_out[...] = jnp.concatenate(lines, axis=0).astype(BF16)


def finish(me, own, rows):
    width = own[0][0].shape[1]
    quarter = rows // 4
    parts = ranges(quarter)
    arrays = [part for packet in own for part in packet]
    any_spec = pl.BlockSpec(memory_space=pl.ANY)
    return pl.pallas_call(
        functools.partial(finish_kernel, rows, parts),
        in_specs=[pl.BlockSpec(memory_space=pltpu.SMEM)] + [any_spec] * len(arrays),
        out_specs=[any_spec, pl.BlockSpec(memory_space=pltpu.VMEM)],
        out_shape=[
            jax.ShapeDtypeStruct((rows, width), BF16),
            jax.ShapeDtypeStruct((4, quarter), BF16),
        ],
        scratch_shapes=[
            pltpu.VMEM((4, TAIL, width), BF16),
            pltpu.SemaphoreType.DMA((len(arrays) + 4,)),
        ],
        compiler_params=pltpu.CompilerParams(vmem_limit_bytes=SMALL_LIMIT),
        name="finish",
    )(me, *arrays)


def per_device(points, block_lists, centroids, dual_weights):
    rows, width = centroids.shape
    quarter = rows // 4
    own_blocks = rows // BLOCK
    position = lax.axis_index("blk")
    groups = lax.axis_size("group")
    member = lax.axis_index("group")
    core, plane = member % 2, member // 2
    me = jnp.stack([core, plane]).astype(jnp.int32)
    target = points.shape[0] * groups / rows
    parts = ranges(quarter)
    whole = [(0, quarter)]
    owner = block_lists // own_blocks
    side = jnp.where(owner == position, 1, jnp.where(owner == position ^ 1, 2, 0))
    near_ids = side * own_blocks + block_lists % own_blocks
    near_ids = near_ids.reshape(-1).astype(jnp.int32)

    def start_packet(c, y):
        first = (c * 2 + y) * quarter
        block = lax.dynamic_slice_in_dim(centroids, first, quarter, 0)
        row = lax.dynamic_slice_in_dim(dual_weights, first, quarter, 0)
        tail = jnp.pad(row[None, :], ((0, TAIL - 1), (0, width - quarter)))
        return jnp.concatenate([block, tail], axis=0)

    def each(move, arrays):
        return [move(a) for a in arrays]

    mine = start_packet(core, plane)
    mine_parts = [mine[a : a + part_rows((a, b), quarter)] for a, b in parts]
    for sweep in range(ITERS):
        near = each(pair_swap, mine_parts)
        far = each(outward, near)
        if sweep == 0:
            beside = start_packet(core, 1 - plane)
            own = [mine, beside, start_packet(1 - core, plane), start_packet(1 - core, 1 - plane)]
        else:
            beside = plane_swap(mine)
            own = [mine, beside, core_swap(mine), core_swap(beside)]
        own = [[packet] for packet in own]
        near_beside = [pair_swap(beside)]
        far_beside = each(plane_swap, far)
        packets = [
            [far, far_beside, each(core_swap, far), each(core_swap, far_beside)],
            own,
            [near, near_beside, each(core_swap, near), each(core_swap, near_beside)],
        ]
        sends, keeps = assign_tiles(points, near_ids, me, packets, rows)
        far_pair, near_pair, own_pair = [(keeps[s], core_swap(sends[s])) for s in (0, 2, 1)]
        far_over = each(plane_swap, add_packets(me, far_pair, [], True, parts))
        near_over = pair_swap(add_packets(me, near_pair, [], True, whole)[0])
        arrived = []
        for part, over in zip(parts, far_over):
            passed = inward(add_packets(me, far_pair, [over], False, [part])[0])
            arrived.append(pair_swap(add_packets(me, near_pair, [passed], False, [part])[0]))
        own_over = plane_swap(add_packets(me, own_pair, [near_over], True, whole)[0])
        last = sweep == ITERS - 1
        renewed = renew(me, mine, *own_pair, own_over, arrived, target, not last)
        mine_parts, mine = renewed[: len(parts)], renewed[-1]
    beside = each(plane_swap, mine_parts)
    own = [mine_parts, beside, each(core_swap, mine_parts), each(core_swap, beside)]
    new_centroids, new_weights = finish(me, own, rows)
    return (new_centroids, new_weights.reshape(rows))


def solution(mesh):
    return jax.shard_map(
        per_device,
        mesh=mesh,
        in_specs=(P(("group", "blk"), None), P(("group", "blk"), None), P("blk", None), P("blk")),
        out_specs=(P("blk", None), P("blk")),
        check_vma=False,
    )
```

```python
import functools

import jax
import jax.numpy as jnp
from jax import lax
from jax.experimental import pallas as pl
from jax.experimental.pallas import tpu as pltpu
from jax.sharding import PartitionSpec as P

BLOCK = 64
TILE = 128
SLOTS = 4
ITERS = 2
TAIL = 16
STEP_TILES = 8
CHUNKS = 2
prior_mass = 1.0
dual_step = 0.5
F32 = jnp.float32
BF16 = jnp.bfloat16
VMEM_LIMIT = 40 * 1024 * 1024
SMALL_LIMIT = 16 * 1024 * 1024


def swap(x, bit):
    groups = lax.axis_size("group")
    return lax.ppermute(x, "group", [(i, i ^ bit) for i in range(groups)])


def core_swap(x):
    return swap(x, 1)


def plane_swap(x):
    return swap(x, 2)


def pair_swap(x):
    count = lax.axis_size("blk")
    return lax.ppermute(x, "blk", [(i, i ^ 1) for i in range(count)])


def cross_swap(x):
    count = lax.axis_size("blk")
    return lax.ppermute(x, "blk", [(i, (i - 1 + i % 2 * 2) % count) for i in range(count)])


def outward(x):
    count = lax.axis_size("blk")
    return lax.ppermute(x, "blk", [(i, (i + 2 - i % 2 * 4) % count) for i in range(count)])


def inward(x):
    count = lax.axis_size("blk")
    return lax.ppermute(x, "blk", [((i + 2 - i % 2 * 4) % count, i) for i in range(count)])


def ranges(quarter):
    size = quarter // CHUNKS
    return [(k * size, (k + 1) * size) for k in range(CHUNKS)]


def part_rows(part, quarter):
    return part[1] - part[0] + (TAIL if part[1] == quarter else 0)


def eye():
    shape = (TILE, TILE)
    return lax.broadcasted_iota(jnp.int32, shape, 0) == lax.broadcasted_iota(jnp.int32, shape, 1)


def to_column(row):
    return jnp.sum(jnp.where(eye(), row, 0.0), axis=1, keepdims=True)


def to_row(column):
    return jnp.sum(jnp.where(eye(), column, 0.0), axis=0, keepdims=True)


def split_masses(row):
    high = row.astype(BF16)
    rest = row - high.astype(F32)
    mid = rest.astype(BF16)
    low = (rest - mid.astype(F32)).astype(BF16)
    return jnp.concatenate([high, mid, low], axis=1)


def tail_of(row):
    wide = jnp.broadcast_to(row.astype(F32), (TAIL, row.shape[1]))
    first = lax.broadcasted_iota(jnp.int32, wide.shape, 0) == 0
    return jnp.where(first, wide, 0.0)


def mass_of(tail, quarter):
    row = tail[0:1, :].astype(F32)
    return row[:, :quarter] + row[:, quarter : 2 * quarter] + row[:, 2 * quarter : 3 * quarter]


def packet_tail(weights, centroids):
    quarter, width = centroids.shape
    rows = []
    for k in range(quarter // TILE):
        base = centroids[k * TILE : (k + 1) * TILE].astype(F32)
        rows.append(to_row(jnp.sum(base * base, axis=1, keepdims=True)))
    offsets = weights - jnp.concatenate(rows, axis=1) * (16.0 / width)
    terms = split_masses(offsets).astype(F32)
    line = lax.broadcasted_iota(jnp.int32, (TAIL, quarter), 0)
    spread = jnp.zeros((TAIL, quarter), F32)
    for k in range(3):
        spread = jnp.where(line == k, terms[:, k * quarter : (k + 1) * quarter], spread)
    first = jnp.where(line == 0, weights, 0.0)
    rest = jnp.zeros((TAIL, width - 2 * quarter), F32)
    return jnp.concatenate([first, spread, rest], axis=1).astype(BF16)


def mass_row(macc, start, quarter):
    ones = jnp.ones((8, TILE), F32)
    rows = [
        lax.dot_general(
            ones,
            macc[pl.ds(start + k * TILE, TILE), :],
            (((1,), (1,)), ((), ())),
            precision=lax.Precision.HIGHEST,
            preferred_element_type=F32,
        )[0:1]
        for k in range(quarter // TILE)
    ]
    return jnp.concatenate(rows, axis=1)


def hand_over(core, rows, sides, acc, macc, sends, keeps):
    quarter = rows // 4
    packet = quarter + TAIL
    half = rows // 2
    for side in range(sides):
        for y in range(2):
            mine = pl.multiple_of(side * rows + core * half + y * quarter, quarter)
            other = pl.multiple_of(side * rows + (1 - core) * half + y * quarter, quarter)
            body = pl.ds(y * packet, quarter)
            tail = pl.ds(y * packet + quarter, TAIL)
            sends[side][body, :] = acc[pl.ds(other, quarter), :].astype(BF16)
            sends[side][tail, :] = tail_of(split_masses(mass_row(macc, other, quarter))).astype(
                BF16
            )
            row = mass_row(macc, mine, quarter)
            keeps[side][body, :] = acc[pl.ds(mine, quarter), :]
            keeps[side][tail, :] = tail_of(jnp.concatenate([row, row * 0.0, row * 0.0], axis=1))


def clear(acc, macc):
    @pl.loop(0, acc.shape[0] // BLOCK)
    def _(b):
        at = pl.ds(pl.multiple_of(b * BLOCK, BLOCK), BLOCK)
        acc[at, :] = jnp.zeros((BLOCK, acc.shape[1]), F32)
        macc[at, :] = jnp.zeros((BLOCK, TILE), F32)


def points_specs(width):
    rows = STEP_TILES * TILE // 2
    return [
        pl.BlockSpec((rows, width), lambda i, ids, me: (2 * i, 0)),
        pl.BlockSpec((rows, width), lambda i, ids, me: (2 * i + 1, 0)),
    ]


def points_of(low, high, t):
    half = STEP_TILES // 2
    return (low if t < half else high)[pl.ds(t % half * TILE, TILE), :]


def tiles_kernel(rows, sizes, ids_ref, me_ref, points_low, points_high, *refs):
    quarter = rows // 4
    count = sum(len(parts) for side in sizes for parts in side)
    parts_refs = list(refs[:count])
    sends = refs[count : count + 3]
    keeps = refs[count + 3 : count + 6]
    near, tails, offs, acc, macc, in_sem = refs[count + 6 :]
    step = pl.program_id(0)
    core = me_ref[0]
    plane = me_ref[1]

    def arrivals():
        out = []
        left = list(parts_refs)
        for side in range(3):
            for j in range(4):
                c = core if j < 2 else 1 - core
                y = plane if j % 2 == 0 else 1 - plane
                at = side * 4 + c * 2 + y
                first = 0
                for size in sizes[side][j]:
                    ref = left.pop(0)
                    last = min(first + size, quarter)
                    out.append(
                        pltpu.make_async_copy(
                            ref.at[pl.ds(0, last - first)],
                            near.at[
                                pl.ds(pl.multiple_of(at * quarter + first, TILE // 2), last - first)
                            ],
                            in_sem.at[len(out)],
                        )
                    )
                    if first + size > quarter:
                        out.append(
                            pltpu.make_async_copy(
                                ref.at[pl.ds(last - first, TAIL)],
                                tails.at[pl.ds(pl.multiple_of(at * TAIL, TAIL), TAIL)],
                                in_sem.at[len(out)],
                            )
                        )
                    first = last
        return out

    width = near.shape[1]

    @pl.when(step == 0)
    def _():
        copies = arrivals()
        for copy in copies:
            copy.start()
        clear(acc, macc)
        for copy in copies:
            copy.wait()
        ones = jnp.ones((TAIL, TILE), BF16)
        for n in range(12):
            for k in range(quarter // TILE):
                terms = tails[n * TAIL : (n + 1) * TAIL, quarter + k * TILE : quarter + (k + 1) * TILE]
                offs[pl.ds(n * quarter + k * TILE, TILE), :] = lax.dot_general(
                    terms, ones, (((0,), (0,)), ((), ())), preferred_element_type=F32
                )

    def blocks_of(t, slots):
        tile = step * STEP_TILES + t
        return [
            pl.ds(pl.multiple_of(ids_ref[tile * SLOTS + k] * BLOCK, BLOCK), BLOCK) for k in slots
        ]

    members = []
    for t in range(STEP_TILES):
        points = points_of(points_low, points_high, t)
        at = blocks_of(t, (0, 2, 1, 3))
        cand = jnp.concatenate([near[a, :] for a in at], axis=0)
        off = jnp.concatenate([offs[a, :] for a in at], axis=0)
        scores = lax.dot_general(
            cand, points, (((1,), (1,)), ((), ())), preferred_element_type=F32
        )
        scores = scores * (32.0 / width) + off
        top = jnp.max(scores, axis=0, keepdims=True)
        raw = jnp.exp(scores - top)
        total = jnp.sum(raw, axis=0, keepdims=True)
        member = (raw * (1.0 / total)).astype(BF16)
        members.append(member)
    for t in range(STEP_TILES):
        points = points_of(points_low, points_high, t)
        at = blocks_of(t, (0, 2, 1, 3))
        numerator = jnp.dot(members[t], points, preferred_element_type=F32)
        masses = members[t].astype(F32)
        for k in range(SLOTS):
            acc[at[k], :] += numerator[k * BLOCK : (k + 1) * BLOCK]
            macc[at[k], :] += masses[k * BLOCK : (k + 1) * BLOCK]

    @pl.when(step == pl.num_programs(0) - 1)
    def _():
        hand_over(core, rows, 3, acc, macc, sends, keeps)


def assign_tiles(points, ids, me, packets, rows):
    count, width = points.shape
    quarter = rows // 4
    packet = quarter + TAIL
    tiles = count // TILE
    any_spec = pl.BlockSpec(memory_space=pl.ANY)
    vmem_spec = pl.BlockSpec(memory_space=pltpu.VMEM)
    step_rows = STEP_TILES * TILE
    sizes = [[[part.shape[0] for part in parts] for parts in side] for side in packets]
    arrays = [part for side in packets for parts in side for part in parts]
    outs = pl.pallas_call(
        functools.partial(tiles_kernel, rows, sizes),
        grid_spec=pltpu.PrefetchScalarGridSpec(
            num_scalar_prefetch=2,
            grid=(tiles // STEP_TILES,),
            in_specs=points_specs(width) + [any_spec] * len(arrays),
            out_specs=[vmem_spec] * 6,
            scratch_shapes=[
                pltpu.VMEM((3 * rows, width), BF16),
                pltpu.VMEM((12 * TAIL, width), BF16),
                pltpu.VMEM((3 * rows, TILE), F32),
                pltpu.VMEM((3 * rows, width), F32),
                pltpu.VMEM((3 * rows, TILE), F32),
                pltpu.SemaphoreType.DMA((len(arrays) + 12,)),
            ],
        ),
        out_shape=[jax.ShapeDtypeStruct((2 * packet, width), BF16)] * 3
        + [jax.ShapeDtypeStruct((2 * packet, width), F32)] * 3,
        compiler_params=pltpu.CompilerParams(vmem_limit_bytes=VMEM_LIMIT),
        cost_estimate=pl.CostEstimate(
            flops=4 * count * SLOTS * BLOCK * width,
            bytes_accessed=2 * count * width,
            transcendentals=count * SLOTS * BLOCK,
        ),
        name="tiles",
    )(ids, me, points, points, *arrays)
    return outs[:3], outs[3:]


def small_call(kernel, me, arrays, outs, name, after=()):
    vmem_spec = pl.BlockSpec(memory_space=pltpu.VMEM)
    return pl.pallas_call(
        kernel,
        in_specs=[pl.BlockSpec(memory_space=pltpu.SMEM)]
        + [vmem_spec] * len(arrays)
        + [pl.BlockSpec(memory_space=pl.ANY)] * len(after),
        out_specs=[vmem_spec] * len(outs),
        out_shape=outs,
        compiler_params=pltpu.CompilerParams(vmem_limit_bytes=SMALL_LIMIT),
        cost_estimate=pl.CostEstimate(
            flops=sum(a.size for a in arrays),
            bytes_accessed=sum(a.size * a.dtype.itemsize for a in arrays),
            transcendentals=0,
        ),
        name=name,
    )(me, *arrays, *after)


def sum_kernel(quarter, pairs, singles, base, outputs, me_ref, *refs):
    terms = refs[: pairs + singles]
    outs = refs[len(refs) - len(outputs) :]

    def rows_of(start, first, size):
        at = [pl.ds(pl.multiple_of(start + first, TAIL), size)] * pairs
        at += [pl.ds(first - base, size)] * singles
        return [term[a, :] for term, a in zip(terms, at)]

    for (over, first, last), out in zip(outputs, outs):
        start = (1 - me_ref[1] if over else me_ref[1]) * (quarter + TAIL)
        size = last - first
        body = rows_of(start, first, size)
        out[pl.ds(0, size), :] = sum(r.astype(F32) for r in body).astype(BF16)
        if last == quarter:
            mass = sum(mass_of(r, quarter) for r in rows_of(start, quarter, TAIL))
            out[pl.ds(size, TAIL), :] = tail_of(split_masses(mass)).astype(BF16)


def add_packets(me, pairs, singles, outputs, base=0, after=()):
    packet, width = pairs[0].shape[0] // 2, pairs[0].shape[1]
    quarter = packet - TAIL
    return small_call(
        functools.partial(sum_kernel, quarter, len(pairs), len(singles), base, outputs),
        me,
        [*pairs, *singles],
        [jax.ShapeDtypeStruct((part_rows(p[1:], quarter), width), BF16) for p in outputs],
        "add_packets",
        after,
    )


def renew_kernel(quarter, target, ranges_in, ranges_out, me_ref, base, keep, beside, *refs):
    terms = list(zip(ranges_in, refs))
    outs = list(zip(ranges_out, refs[len(terms) :]))
    start = me_ref[1] * (quarter + TAIL)
    mass = sum(
        mass_of(ref[pl.ds(last - first, TAIL), :], quarter)
        for (first, last), ref in terms
        if last == quarter
    )
    for term in (keep, beside):
        tail = term[pl.ds(pl.multiple_of(start + quarter, TAIL), TAIL), :]
        mass = mass + mass_of(tail, quarter)
    weights = base[pl.ds(quarter, TAIL), :].astype(F32)[0:1, :quarter]
    renewed = weights + dual_step * (1.0 - mass / target)
    renewed = renewed.astype(BF16).astype(F32)
    blocks = []
    for row in range(0, quarter, TILE):
        here = pl.ds(pl.multiple_of(start + row, TAIL), TILE)
        total = keep[here, :] + beside[here, :].astype(F32)
        for (first, last), ref in terms:
            if first <= row < last:
                total = total + ref[pl.ds(row - first, TILE), :].astype(F32)
        column = to_column(mass[:, row : row + TILE]) + prior_mass
        total = total + prior_mass * base[pl.ds(row, TILE), :].astype(F32)
        blocks.append((total / column).astype(BF16))
    tail = packet_tail(renewed, jnp.concatenate(blocks, axis=0))
    for (first, last), out in outs:
        for row in range(first, last, TILE):
            out[pl.ds(row - first, TILE), :] = blocks[row // TILE]
        if last == quarter:
            out[pl.ds(last - first, TAIL), :] = tail


def renew(me, base, pair, terms, ranges_in, target, ranges_out):
    packet, width = base.shape
    quarter = packet - TAIL
    return small_call(
        functools.partial(renew_kernel, quarter, target, ranges_in, ranges_out),
        me,
        [base, *pair, *terms],
        [jax.ShapeDtypeStruct((part_rows(p, quarter), width), BF16) for p in ranges_out],
        "renew",
    )


def start_kernel(quarter, which, me_ref, centroids, weights, *refs):
    outs = refs[: len(which)]
    block, sem = refs[len(which) :]
    core, plane = me_ref[0], me_ref[1]
    places = []
    for c, y, first, last in which:
        if (c, y) not in places:
            places.append((c, y))
    copies = []
    for n, (c, y) in enumerate(places):
        place = (core if c else 1 - core) * 2 + (plane if y else 1 - plane)
        at = pl.multiple_of(place * quarter, quarter)
        copies.append(
            pltpu.make_async_copy(centroids.at[pl.ds(at, quarter)], block.at[n], sem.at[n])
        )
        copies[-1].start()
    for n, (c, y) in enumerate(places):
        place = (core if c else 1 - core) * 2 + (plane if y else 1 - plane)
        lines = jnp.zeros((1, quarter), F32)
        for q in range(4):
            lines = jnp.where(place == q, weights[q : q + 1, :].astype(F32), lines)
        copies[n].wait()
        rows = block[n]
        tail = packet_tail(lines, rows)
        for (oc, oy, first, last), out in zip(which, outs):
            if (oc, oy) == (c, y):
                out[pl.ds(0, last - first), :] = rows[first:last]
                if last == quarter:
                    out[pl.ds(last - first, TAIL), :] = tail


def start_packets(me, centroids, weights, which):
    rows, width = centroids.shape
    quarter = rows // 4
    vmem_spec = pl.BlockSpec(memory_space=pltpu.VMEM)
    return pl.pallas_call(
        functools.partial(start_kernel, quarter, which),
        in_specs=[
            pl.BlockSpec(memory_space=pltpu.SMEM),
            pl.BlockSpec(memory_space=pltpu.HBM),
            vmem_spec,
        ],
        out_specs=[vmem_spec] * len(which),
        out_shape=[
            jax.ShapeDtypeStruct((part_rows(p[2:], quarter), width), BF16) for p in which
        ],
        scratch_shapes=[pltpu.VMEM((3, quarter, width), BF16), pltpu.SemaphoreType.DMA((3,))],
        compiler_params=pltpu.CompilerParams(vmem_limit_bytes=SMALL_LIMIT),
        name="start_packets",
    )(me, centroids, weights)


def finish_kernel(rows, parts, me_ref, *refs):
    quarter = rows // 4
    n = 4 * len(parts)
    packets = refs[:n]
    out, weights_out, tails, sem = refs[n:]
    core, plane = me_ref[0], me_ref[1]
    copies = []
    places = []
    for j in range(4):
        c = core if j < 2 else 1 - core
        y = plane if j % 2 == 0 else 1 - plane
        places.append(c * 2 + y)
        for k, (first, last) in enumerate(parts):
            ref = packets[j * len(parts) + k]
            at = pl.multiple_of(places[j] * quarter + first, TILE)
            copies.append(
                pltpu.make_async_copy(
                    ref.at[pl.ds(0, last - first)],
                    out.at[pl.ds(at, last - first)],
                    sem.at[len(copies)],
                )
            )
            if last == quarter:
                copies.append(
                    pltpu.make_async_copy(
                        ref.at[pl.ds(last - first, TAIL)], tails.at[j], sem.at[len(copies)]
                    )
                )
    for copy in copies:
        copy.start()
    for copy in copies:
        copy.wait()
    found = [tails[j][0:1, :quarter].astype(F32) for j in range(4)]
    lines = []
    for q in range(4):
        line = found[0]
        for j in range(1, 4):
            line = jnp.where(places[j] == q, found[j], line)
        lines.append(line)
    weights_out[...] = jnp.concatenate(lines, axis=0).astype(BF16)


def finish(me, own, rows):
    width = own[0][0].shape[1]
    quarter = rows // 4
    parts = ranges(quarter)
    arrays = [part for packet in own for part in packet]
    any_spec = pl.BlockSpec(memory_space=pl.ANY)
    return pl.pallas_call(
        functools.partial(finish_kernel, rows, parts),
        in_specs=[pl.BlockSpec(memory_space=pltpu.SMEM)] + [any_spec] * len(arrays),
        out_specs=[any_spec, pl.BlockSpec(memory_space=pltpu.VMEM)],
        out_shape=[
            jax.ShapeDtypeStruct((rows, width), BF16),
            jax.ShapeDtypeStruct((4, quarter), BF16),
        ],
        scratch_shapes=[
            pltpu.VMEM((4, TAIL, width), BF16),
            pltpu.SemaphoreType.DMA((len(arrays) + 4,)),
        ],
        compiler_params=pltpu.CompilerParams(vmem_limit_bytes=SMALL_LIMIT),
        name="finish",
    )(me, *arrays)


def per_device(points, block_lists, centroids, dual_weights):
    rows, width = centroids.shape
    quarter = rows // 4
    own_blocks = rows // BLOCK
    position = lax.axis_index("blk")
    groups = lax.axis_size("group")
    member = lax.axis_index("group")
    core, plane = member % 2, member // 2
    me = jnp.stack([core, plane]).astype(jnp.int32)
    target = points.shape[0] * groups / rows
    parts = ranges(quarter)
    owner = block_lists // own_blocks
    side = jnp.where(owner == position, 2, jnp.where(owner == position ^ 1, 1, 0))
    near_ids = side * own_blocks + block_lists % own_blocks
    near_ids = near_ids.reshape(-1).astype(jnp.int32)

    def each(move, arrays):
        return [move(a) for a in arrays]

    lines = dual_weights.reshape(4, quarter)
    everything = (0, quarter)
    low, high = parts
    [mine] = start_packets(me, centroids, lines, [(1, 1, *everything)])
    for sweep in range(ITERS):
        far, near = cross_swap(mine), pair_swap(mine)
        if sweep == 0:
            which = [(c, y, *everything) for c, y in ((1, 0), (0, 1), (0, 0))]
            own = [mine, *start_packets(me, centroids, lines, which)]
            beside = own[1]
        else:
            beside = plane_swap(mine)
            own = [mine, beside, core_swap(mine), core_swap(beside)]
        near_beside = pair_swap(beside)
        far_beside = plane_swap(far)
        packets = [
            [far, far_beside, core_swap(far), core_swap(far_beside)],
            [near, near_beside, core_swap(near), core_swap(near_beside)],
            own,
        ]
        packets = [[[packet] for packet in side] for side in packets]
        sends, keeps = assign_tiles(points, near_ids, me, packets, rows)
        far_pair, near_pair, own_pair = [(k, core_swap(a)) for a, k in zip(sends, keeps)]
        far_sums = add_packets(me, far_pair, [], [(True, *high), (True, *low)])
        far_over_high, far_over_low = each(plane_swap, far_sums)
        near_sums = add_packets(
            me, near_pair, [], [(True, *low), (True, *high), (False, *low)]
        )
        near_over_low, near_over_high, near_here_low = each(pair_swap, near_sums)
        [far_high] = add_packets(
            me, far_pair, [far_over_high], [(False, *high)], high[0], [near_over_low]
        )
        far_high = inward(far_high)
        [far_low] = add_packets(
            me, far_pair, [far_over_low], [(False, *low)], low[0], [near_over_high]
        )
        far_here_low = cross_swap(far_low)
        own_low = add_packets(me, own_pair, [near_over_low], [(True, *low)], low[0])
        own_high = add_packets(me, own_pair, [near_over_high], [(True, *high)], high[0])
        own_over_low, own_over_high = each(plane_swap, [*own_low, *own_high])
        [near_high] = add_packets(
            me,
            near_pair,
            [far_high],
            [(False, *high)],
            high[0],
            [near_here_low, *own_low, *own_high],
        )
        near_here_high = pair_swap(near_high)
        last = sweep == ITERS - 1
        mine_parts = renew(
            me,
            mine,
            own_pair,
            [own_over_low, own_over_high, near_here_low, near_here_high, far_here_low],
            [low, high, low, high, low],
            target,
            parts if last else [everything],
        )
        mine = mine_parts[0]
    beside = each(plane_swap, mine_parts)
    own = [mine_parts, beside, each(core_swap, mine_parts), each(core_swap, beside)]
    new_centroids, new_weights = finish(me, own, rows)
    return (new_centroids, new_weights.reshape(rows))


def solution(mesh):
    return jax.shard_map(
        per_device,
        mesh=mesh,
        in_specs=(P(("group", "blk"), None), P(("group", "blk"), None), P("blk", None), P("blk")),
        out_specs=(P("blk", None), P("blk")),
        check_vma=False,
    )
```

```python
import functools

import jax
import jax.numpy as jnp
from jax import lax
from jax.experimental import pallas as pl
from jax.experimental.pallas import tpu as pltpu
from jax.sharding import PartitionSpec as P

BLOCK = 64
TILE = 128
SLOTS = 4
ITERS = 2
TAIL = 16
STEP_TILES = 8
CHUNKS = 2
prior_mass = 1.0
dual_step = 0.5
F32 = jnp.float32
BF16 = jnp.bfloat16
VMEM_LIMIT = 40 * 1024 * 1024
SMALL_LIMIT = 16 * 1024 * 1024


def swap(x, bit):
    groups = lax.axis_size("group")
    return lax.ppermute(x, "group", [(i, i ^ bit) for i in range(groups)])


def core_swap(x):
    return swap(x, 1)


def plane_swap(x):
    return swap(x, 2)


def pair_swap(x):
    count = lax.axis_size("blk")
    return lax.ppermute(x, "blk", [(i, i ^ 1) for i in range(count)])


def cross_swap(x):
    count = lax.axis_size("blk")
    return lax.ppermute(x, "blk", [(i, (i - 1 + i % 2 * 2) % count) for i in range(count)])


def outward(x):
    count = lax.axis_size("blk")
    return lax.ppermute(x, "blk", [(i, (i + 2 - i % 2 * 4) % count) for i in range(count)])


def inward(x):
    count = lax.axis_size("blk")
    return lax.ppermute(x, "blk", [((i + 2 - i % 2 * 4) % count, i) for i in range(count)])


def ranges(quarter):
    size = quarter // CHUNKS
    return [(k * size, (k + 1) * size) for k in range(CHUNKS)]


def part_rows(part, quarter):
    return part[1] - part[0] + (TAIL if part[1] == quarter else 0)


def eye():
    shape = (TILE, TILE)
    return lax.broadcasted_iota(jnp.int32, shape, 0) == lax.broadcasted_iota(jnp.int32, shape, 1)


def to_column(row):
    return jnp.sum(jnp.where(eye(), row, 0.0), axis=1, keepdims=True)


def to_row(column):
    return jnp.sum(jnp.where(eye(), column, 0.0), axis=0, keepdims=True)


def split_masses(row):
    high = row.astype(BF16)
    rest = row - high.astype(F32)
    mid = rest.astype(BF16)
    low = (rest - mid.astype(F32)).astype(BF16)
    return jnp.concatenate([high, mid, low], axis=1)


def tail_of(row):
    wide = jnp.broadcast_to(row.astype(F32), (TAIL, row.shape[1]))
    first = lax.broadcasted_iota(jnp.int32, wide.shape, 0) == 0
    return jnp.where(first, wide, 0.0)


def mass_of(tail, quarter):
    row = tail[0:1, :].astype(F32)
    return row[:, :quarter] + row[:, quarter : 2 * quarter] + row[:, 2 * quarter : 3 * quarter]


def packet_tail(weights, centroids):
    quarter, width = centroids.shape
    rows = []
    for k in range(quarter // TILE):
        base = centroids[k * TILE : (k + 1) * TILE].astype(F32)
        rows.append(to_row(jnp.sum(base * base, axis=1, keepdims=True)))
    offsets = weights - jnp.concatenate(rows, axis=1) * (16.0 / width)
    terms = split_masses(offsets).astype(F32)
    line = lax.broadcasted_iota(jnp.int32, (TAIL, quarter), 0)
    spread = jnp.zeros((TAIL, quarter), F32)
    for k in range(3):
        spread = jnp.where(line == k, terms[:, k * quarter : (k + 1) * quarter], spread)
    first = jnp.where(line == 0, weights, 0.0)
    rest = jnp.zeros((TAIL, width - 2 * quarter), F32)
    return jnp.concatenate([first, spread, rest], axis=1).astype(BF16)


def mass_row(macc, start, quarter):
    ones = jnp.ones((8, TILE), F32)
    rows = [
        lax.dot_general(
            ones,
            macc[pl.ds(start + k * TILE, TILE), :],
            (((1,), (1,)), ((), ())),
            precision=lax.Precision.HIGHEST,
            preferred_element_type=F32,
        )[0:1]
        for k in range(quarter // TILE)
    ]
    return jnp.concatenate(rows, axis=1)


def hand_over(core, rows, sides, acc, macc, sends, keeps):
    quarter = rows // 4
    packet = quarter + TAIL
    half = rows // 2
    for side in range(sides):
        for y in range(2):
            mine = pl.multiple_of(side * rows + core * half + y * quarter, quarter)
            other = pl.multiple_of(side * rows + (1 - core) * half + y * quarter, quarter)
            body = pl.ds(y * packet, quarter)
            tail = pl.ds(y * packet + quarter, TAIL)
            sends[side][body, :] = acc[pl.ds(other, quarter), :].astype(BF16)
            sends[side][tail, :] = tail_of(split_masses(mass_row(macc, other, quarter))).astype(
                BF16
            )
            row = mass_row(macc, mine, quarter)
            keeps[side][body, :] = acc[pl.ds(mine, quarter), :]
            keeps[side][tail, :] = tail_of(jnp.concatenate([row, row * 0.0, row * 0.0], axis=1))


def clear(acc, macc):
    @pl.loop(0, acc.shape[0] // BLOCK)
    def _(b):
        at = pl.ds(pl.multiple_of(b * BLOCK, BLOCK), BLOCK)
        acc[at, :] = jnp.zeros((BLOCK, acc.shape[1]), F32)
        macc[at, :] = jnp.zeros((BLOCK, TILE), F32)


def tiles_kernel(rows, sizes, ids_ref, me_ref, points_ref, *refs):
    quarter = rows // 4
    count = sum(len(parts) for side in sizes for parts in side)
    parts_refs = list(refs[:count])
    sends = refs[count : count + 3]
    keeps = refs[count + 3 : count + 6]
    near, tails, offs, acc, macc, held, in_sem, held_sem = refs[count + 6 :]
    step = pl.program_id(0)
    core = me_ref[0]
    plane = me_ref[1]

    def arrivals():
        out = []
        left = list(parts_refs)
        for side in range(3):
            for j in range(4):
                c = core if j < 2 else 1 - core
                y = plane if j % 2 == 0 else 1 - plane
                at = side * 4 + c * 2 + y
                first = 0
                for size in sizes[side][j]:
                    ref = left.pop(0)
                    last = min(first + size, quarter)
                    out.append(
                        pltpu.make_async_copy(
                            ref.at[pl.ds(0, last - first)],
                            near.at[
                                pl.ds(pl.multiple_of(at * quarter + first, TILE // 2), last - first)
                            ],
                            in_sem.at[len(out)],
                        )
                    )
                    if first + size > quarter:
                        out.append(
                            pltpu.make_async_copy(
                                ref.at[pl.ds(last - first, TAIL)],
                                tails.at[pl.ds(pl.multiple_of(at * TAIL, TAIL), TAIL)],
                                in_sem.at[len(out)],
                            )
                        )
                    first = last
        return out

    width = near.shape[1]
    step_rows = STEP_TILES * TILE

    def points_copy(n):
        at = pl.ds(pl.multiple_of(n * step_rows, step_rows), step_rows)
        return pltpu.make_async_copy(points_ref.at[at], held.at[at], held_sem.at[n])

    def rows_at(t):
        return pl.ds(pl.multiple_of(step * step_rows + t * TILE, TILE), TILE)

    @pl.when(step == 0)
    def _():
        copies = arrivals()
        for copy in copies:
            copy.start()
        for n in range(held.shape[0] // step_rows):
            points_copy(n).start()
        clear(acc, macc)
        for copy in copies:
            copy.wait()
        ones = jnp.ones((TAIL, TILE), BF16)
        for n in range(12):
            for k in range(quarter // TILE):
                terms = tails[n * TAIL : (n + 1) * TAIL, quarter + k * TILE : quarter + (k + 1) * TILE]
                offs[pl.ds(n * quarter + k * TILE, TILE), :] = lax.dot_general(
                    terms, ones, (((0,), (0,)), ((), ())), preferred_element_type=F32
                )

    def blocks_of(t, slots):
        tile = step * STEP_TILES + t
        return [
            pl.ds(pl.multiple_of(ids_ref[tile * SLOTS + k] * BLOCK, BLOCK), BLOCK) for k in slots
        ]

    points_copy(step).wait()
    members = []
    for t in range(STEP_TILES):
        points = held[rows_at(t), :]
        at = blocks_of(t, (0, 2, 1, 3))
        cand = jnp.concatenate([near[a, :] for a in at], axis=0)
        off = jnp.concatenate([offs[a, :] for a in at], axis=0)
        scores = lax.dot_general(
            cand, points, (((1,), (1,)), ((), ())), preferred_element_type=F32
        )
        scores = scores * (32.0 / width) + off
        top = jnp.max(scores, axis=0, keepdims=True)
        raw = jnp.exp(scores - top)
        total = jnp.sum(raw, axis=0, keepdims=True)
        member = (raw * (1.0 / total)).astype(BF16)
        members.append(member)
    for t in range(STEP_TILES):
        points = held[rows_at(t), :]
        at = blocks_of(t, (0, 2, 1, 3))
        numerator = jnp.dot(members[t], points, preferred_element_type=F32)
        masses = members[t].astype(F32)
        for k in range(SLOTS):
            acc[at[k], :] += numerator[k * BLOCK : (k + 1) * BLOCK]
            macc[at[k], :] += masses[k * BLOCK : (k + 1) * BLOCK]

    @pl.when(step == pl.num_programs(0) - 1)
    def _():
        hand_over(core, rows, 3, acc, macc, sends, keeps)


def assign_tiles(points, ids, me, packets, rows):
    count, width = points.shape
    quarter = rows // 4
    packet = quarter + TAIL
    tiles = count // TILE
    any_spec = pl.BlockSpec(memory_space=pl.ANY)
    vmem_spec = pl.BlockSpec(memory_space=pltpu.VMEM)
    step_rows = STEP_TILES * TILE
    sizes = [[[part.shape[0] for part in parts] for parts in side] for side in packets]
    arrays = [part for side in packets for parts in side for part in parts]
    outs = pl.pallas_call(
        functools.partial(tiles_kernel, rows, sizes),
        grid_spec=pltpu.PrefetchScalarGridSpec(
            num_scalar_prefetch=2,
            grid=(tiles // STEP_TILES,),
            in_specs=[pl.BlockSpec(memory_space=pltpu.HBM)] + [any_spec] * len(arrays),
            out_specs=[vmem_spec] * 6,
            scratch_shapes=[
                pltpu.VMEM((3 * rows, width), BF16),
                pltpu.VMEM((12 * TAIL, width), BF16),
                pltpu.VMEM((3 * rows, TILE), F32),
                pltpu.VMEM((3 * rows, width), F32),
                pltpu.VMEM((3 * rows, TILE), F32),
                pltpu.VMEM((count, width), BF16),
                pltpu.SemaphoreType.DMA((len(arrays) + 12,)),
                pltpu.SemaphoreType.DMA((tiles // STEP_TILES,)),
            ],
        ),
        out_shape=[jax.ShapeDtypeStruct((2 * packet, width), BF16)] * 3
        + [jax.ShapeDtypeStruct((2 * packet, width), F32)] * 3,
        compiler_params=pltpu.CompilerParams(vmem_limit_bytes=VMEM_LIMIT),
        cost_estimate=pl.CostEstimate(
            flops=4 * count * SLOTS * BLOCK * width,
            bytes_accessed=2 * count * width,
            transcendentals=count * SLOTS * BLOCK,
        ),
        name="tiles",
    )(ids, me, points, *arrays)
    return outs[:3], outs[3:]


def small_call(kernel, me, arrays, outs, name, after=()):
    vmem_spec = pl.BlockSpec(memory_space=pltpu.VMEM)
    return pl.pallas_call(
        kernel,
        in_specs=[pl.BlockSpec(memory_space=pltpu.SMEM)]
        + [vmem_spec] * len(arrays)
        + [pl.BlockSpec(memory_space=pl.ANY)] * len(after),
        out_specs=[vmem_spec] * len(outs),
        out_shape=outs,
        compiler_params=pltpu.CompilerParams(vmem_limit_bytes=SMALL_LIMIT),
        cost_estimate=pl.CostEstimate(
            flops=sum(a.size for a in arrays),
            bytes_accessed=sum(a.size * a.dtype.itemsize for a in arrays),
            transcendentals=0,
        ),
        name=name,
    )(me, *arrays, *after)


def sum_kernel(quarter, pairs, singles, base, outputs, me_ref, *refs):
    terms = refs[: pairs + singles]
    outs = refs[len(refs) - len(outputs) :]

    def rows_of(start, first, size):
        at = [pl.ds(pl.multiple_of(start + first, TAIL), size)] * pairs
        at += [pl.ds(first - base, size)] * singles
        return [term[a, :] for term, a in zip(terms, at)]

    for (over, first, last), out in zip(outputs, outs):
        start = (1 - me_ref[1] if over else me_ref[1]) * (quarter + TAIL)
        size = last - first
        body = rows_of(start, first, size)
        out[pl.ds(0, size), :] = sum(r.astype(F32) for r in body).astype(BF16)
        if last == quarter:
            mass = sum(mass_of(r, quarter) for r in rows_of(start, quarter, TAIL))
            out[pl.ds(size, TAIL), :] = tail_of(split_masses(mass)).astype(BF16)


def add_packets(me, pairs, singles, outputs, base=0, after=()):
    packet, width = pairs[0].shape[0] // 2, pairs[0].shape[1]
    quarter = packet - TAIL
    return small_call(
        functools.partial(sum_kernel, quarter, len(pairs), len(singles), base, outputs),
        me,
        [*pairs, *singles],
        [jax.ShapeDtypeStruct((part_rows(p[1:], quarter), width), BF16) for p in outputs],
        "add_packets",
        after,
    )


def renew_kernel(quarter, target, ranges_in, ranges_out, me_ref, base, keep, beside, *refs):
    terms = list(zip(ranges_in, refs))
    outs = list(zip(ranges_out, refs[len(terms) :]))
    start = me_ref[1] * (quarter + TAIL)
    mass = sum(
        mass_of(ref[pl.ds(last - first, TAIL), :], quarter)
        for (first, last), ref in terms
        if last == quarter
    )
    for term in (keep, beside):
        tail = term[pl.ds(pl.multiple_of(start + quarter, TAIL), TAIL), :]
        mass = mass + mass_of(tail, quarter)
    weights = base[pl.ds(quarter, TAIL), :].astype(F32)[0:1, :quarter]
    renewed = weights + dual_step * (1.0 - mass / target)
    renewed = renewed.astype(BF16).astype(F32)
    blocks = []
    for row in range(0, quarter, TILE):
        here = pl.ds(pl.multiple_of(start + row, TAIL), TILE)
        total = keep[here, :] + beside[here, :].astype(F32)
        for (first, last), ref in terms:
            if first <= row < last:
                total = total + ref[pl.ds(row - first, TILE), :].astype(F32)
        column = to_column(mass[:, row : row + TILE]) + prior_mass
        total = total + prior_mass * base[pl.ds(row, TILE), :].astype(F32)
        blocks.append((total / column).astype(BF16))
    tail = packet_tail(renewed, jnp.concatenate(blocks, axis=0))
    for (first, last), out in outs:
        for row in range(first, last, TILE):
            out[pl.ds(row - first, TILE), :] = blocks[row // TILE]
        if last == quarter:
            out[pl.ds(last - first, TAIL), :] = tail


def renew(me, base, pair, terms, ranges_in, target, ranges_out):
    packet, width = base.shape
    quarter = packet - TAIL
    return small_call(
        functools.partial(renew_kernel, quarter, target, ranges_in, ranges_out),
        me,
        [base, *pair, *terms],
        [jax.ShapeDtypeStruct((part_rows(p, quarter), width), BF16) for p in ranges_out],
        "renew",
    )


def start_kernel(quarter, which, me_ref, centroids, weights, *refs):
    outs = refs[: len(which)]
    block, sem = refs[len(which) :]
    core, plane = me_ref[0], me_ref[1]
    places = []
    for c, y, first, last in which:
        if (c, y) not in places:
            places.append((c, y))
    copies = []
    for n, (c, y) in enumerate(places):
        place = (core if c else 1 - core) * 2 + (plane if y else 1 - plane)
        at = pl.multiple_of(place * quarter, quarter)
        copies.append(
            pltpu.make_async_copy(centroids.at[pl.ds(at, quarter)], block.at[n], sem.at[n])
        )
        copies[-1].start()
    for n, (c, y) in enumerate(places):
        place = (core if c else 1 - core) * 2 + (plane if y else 1 - plane)
        lines = jnp.zeros((1, quarter), F32)
        for q in range(4):
            lines = jnp.where(place == q, weights[q : q + 1, :].astype(F32), lines)
        copies[n].wait()
        rows = block[n]
        tail = packet_tail(lines, rows)
        for (oc, oy, first, last), out in zip(which, outs):
            if (oc, oy) == (c, y):
                out[pl.ds(0, last - first), :] = rows[first:last]
                if last == quarter:
                    out[pl.ds(last - first, TAIL), :] = tail


def start_packets(me, centroids, weights, which):
    rows, width = centroids.shape
    quarter = rows // 4
    vmem_spec = pl.BlockSpec(memory_space=pltpu.VMEM)
    return pl.pallas_call(
        functools.partial(start_kernel, quarter, which),
        in_specs=[
            pl.BlockSpec(memory_space=pltpu.SMEM),
            pl.BlockSpec(memory_space=pltpu.HBM),
            vmem_spec,
        ],
        out_specs=[vmem_spec] * len(which),
        out_shape=[
            jax.ShapeDtypeStruct((part_rows(p[2:], quarter), width), BF16) for p in which
        ],
        scratch_shapes=[pltpu.VMEM((3, quarter, width), BF16), pltpu.SemaphoreType.DMA((3,))],
        compiler_params=pltpu.CompilerParams(vmem_limit_bytes=SMALL_LIMIT),
        name="start_packets",
    )(me, centroids, weights)


def finish_kernel(rows, parts, me_ref, *refs):
    quarter = rows // 4
    n = 4 * len(parts)
    packets = refs[:n]
    out, weights_out, tails, sem = refs[n:]
    core, plane = me_ref[0], me_ref[1]
    copies = []
    places = []
    for j in range(4):
        c = core if j < 2 else 1 - core
        y = plane if j % 2 == 0 else 1 - plane
        places.append(c * 2 + y)
        for k, (first, last) in enumerate(parts):
            ref = packets[j * len(parts) + k]
            at = pl.multiple_of(places[j] * quarter + first, TILE)
            copies.append(
                pltpu.make_async_copy(
                    ref.at[pl.ds(0, last - first)],
                    out.at[pl.ds(at, last - first)],
                    sem.at[len(copies)],
                )
            )
            if last == quarter:
                copies.append(
                    pltpu.make_async_copy(
                        ref.at[pl.ds(last - first, TAIL)], tails.at[j], sem.at[len(copies)]
                    )
                )
    for copy in copies:
        copy.start()
    for copy in copies:
        copy.wait()
    found = [tails[j][0:1, :quarter].astype(F32) for j in range(4)]
    lines = []
    for q in range(4):
        line = found[0]
        for j in range(1, 4):
            line = jnp.where(places[j] == q, found[j], line)
        lines.append(line)
    weights_out[...] = jnp.concatenate(lines, axis=0).astype(BF16)


def finish(me, own, rows):
    width = own[0][0].shape[1]
    quarter = rows // 4
    parts = ranges(quarter)
    arrays = [part for packet in own for part in packet]
    any_spec = pl.BlockSpec(memory_space=pl.ANY)
    return pl.pallas_call(
        functools.partial(finish_kernel, rows, parts),
        in_specs=[pl.BlockSpec(memory_space=pltpu.SMEM)] + [any_spec] * len(arrays),
        out_specs=[any_spec, pl.BlockSpec(memory_space=pltpu.VMEM)],
        out_shape=[
            jax.ShapeDtypeStruct((rows, width), BF16),
            jax.ShapeDtypeStruct((4, quarter), BF16),
        ],
        scratch_shapes=[
            pltpu.VMEM((4, TAIL, width), BF16),
            pltpu.SemaphoreType.DMA((len(arrays) + 4,)),
        ],
        compiler_params=pltpu.CompilerParams(vmem_limit_bytes=SMALL_LIMIT),
        name="finish",
    )(me, *arrays)


def per_device(points, block_lists, centroids, dual_weights):
    rows, width = centroids.shape
    quarter = rows // 4
    own_blocks = rows // BLOCK
    position = lax.axis_index("blk")
    groups = lax.axis_size("group")
    member = lax.axis_index("group")
    core, plane = member % 2, member // 2
    me = jnp.stack([core, plane]).astype(jnp.int32)
    target = points.shape[0] * groups / rows
    parts = ranges(quarter)
    owner = block_lists // own_blocks
    side = jnp.where(owner == position, 2, jnp.where(owner == position ^ 1, 1, 0))
    near_ids = side * own_blocks + block_lists % own_blocks
    near_ids = near_ids.reshape(-1).astype(jnp.int32)

    def each(move, arrays):
        return [move(a) for a in arrays]

    lines = dual_weights.reshape(4, quarter)
    everything = (0, quarter)
    low, high = parts
    [mine] = start_packets(me, centroids, lines, [(1, 1, *everything)])
    for sweep in range(ITERS):
        far, near = cross_swap(mine), pair_swap(mine)
        if sweep == 0:
            which = [(c, y, *everything) for c, y in ((1, 0), (0, 1), (0, 0))]
            own = [mine, *start_packets(me, centroids, lines, which)]
            beside = own[1]
        else:
            beside = plane_swap(mine)
            own = [mine, beside, core_swap(mine), core_swap(beside)]
        near_beside = pair_swap(beside)
        far_beside = plane_swap(far)
        packets = [
            [far, far_beside, core_swap(far), core_swap(far_beside)],
            [near, near_beside, core_swap(near), core_swap(near_beside)],
            own,
        ]
        packets = [[[packet] for packet in side] for side in packets]
        sends, keeps = assign_tiles(points, near_ids, me, packets, rows)
        far_pair, near_pair, own_pair = [(k, core_swap(a)) for a, k in zip(sends, keeps)]
        far_sums = add_packets(me, far_pair, [], [(True, *high), (True, *low)])
        far_over_high, far_over_low = each(plane_swap, far_sums)
        near_sums = add_packets(
            me, near_pair, [], [(True, *low), (True, *high), (False, *low)]
        )
        near_over_low, near_over_high, near_here_low = each(pair_swap, near_sums)
        [far_high] = add_packets(
            me, far_pair, [far_over_high], [(False, *high)], high[0], [near_over_low]
        )
        far_high = inward(far_high)
        [far_low] = add_packets(
            me, far_pair, [far_over_low], [(False, *low)], low[0], [near_over_high]
        )
        far_here_low = cross_swap(far_low)
        own_low = add_packets(me, own_pair, [near_over_low], [(True, *low)], low[0])
        own_high = add_packets(me, own_pair, [near_over_high], [(True, *high)], high[0])
        own_over_low, own_over_high = each(plane_swap, [*own_low, *own_high])
        [near_high] = add_packets(
            me,
            near_pair,
            [far_high],
            [(False, *high)],
            high[0],
            [near_here_low, *own_low, *own_high],
        )
        near_here_high = pair_swap(near_high)
        last = sweep == ITERS - 1
        mine_parts = renew(
            me,
            mine,
            own_pair,
            [own_over_low, own_over_high, near_here_low, near_here_high, far_here_low],
            [low, high, low, high, low],
            target,
            parts if last else [everything],
        )
        mine = mine_parts[0]
    beside = each(plane_swap, mine_parts)
    own = [mine_parts, beside, each(core_swap, mine_parts), each(core_swap, beside)]
    new_centroids, new_weights = finish(me, own, rows)
    return (new_centroids, new_weights.reshape(rows))


def solution(mesh):
    return jax.shard_map(
        per_device,
        mesh=mesh,
        in_specs=(P(("group", "blk"), None), P(("group", "blk"), None), P("blk", None), P("blk")),
        out_specs=(P("blk", None), P("blk")),
        check_vma=False,
    )
```

```python
import functools

import jax
import jax.numpy as jnp
from jax import lax
from jax.experimental import pallas as pl
from jax.experimental.pallas import tpu as pltpu
from jax.sharding import PartitionSpec as P

BLOCK = 64
TILE = 128
SLOTS = 4
ITERS = 2
TAIL = 16
STEP_TILES = 16
CHUNKS = 2
prior_mass = 1.0
dual_step = 0.5
F32 = jnp.float32
BF16 = jnp.bfloat16
VMEM_LIMIT = 40 * 1024 * 1024
SMALL_LIMIT = 16 * 1024 * 1024


def swap(x, bit):
    groups = lax.axis_size("group")
    return lax.ppermute(x, "group", [(i, i ^ bit) for i in range(groups)])


def core_swap(x):
    return swap(x, 1)


def plane_swap(x):
    return swap(x, 2)


def pair_swap(x):
    count = lax.axis_size("blk")
    return lax.ppermute(x, "blk", [(i, i ^ 1) for i in range(count)])


def cross_swap(x):
    count = lax.axis_size("blk")
    return lax.ppermute(x, "blk", [(i, (i - 1 + i % 2 * 2) % count) for i in range(count)])


def outward(x):
    count = lax.axis_size("blk")
    return lax.ppermute(x, "blk", [(i, (i + 2 - i % 2 * 4) % count) for i in range(count)])


def inward(x):
    count = lax.axis_size("blk")
    return lax.ppermute(x, "blk", [((i + 2 - i % 2 * 4) % count, i) for i in range(count)])


def ranges(quarter):
    size = quarter // CHUNKS
    return [(k * size, (k + 1) * size) for k in range(CHUNKS)]


def part_rows(part, quarter):
    return part[1] - part[0] + (TAIL if part[1] == quarter else 0)


def eye():
    shape = (TILE, TILE)
    return lax.broadcasted_iota(jnp.int32, shape, 0) == lax.broadcasted_iota(jnp.int32, shape, 1)


def to_column(row):
    return jnp.sum(jnp.where(eye(), row, 0.0), axis=1, keepdims=True)


def to_row(column):
    return jnp.sum(jnp.where(eye(), column, 0.0), axis=0, keepdims=True)


def split_masses(row):
    high = row.astype(BF16)
    rest = row - high.astype(F32)
    mid = rest.astype(BF16)
    low = (rest - mid.astype(F32)).astype(BF16)
    return jnp.concatenate([high, mid, low], axis=1)


def tail_of(row):
    wide = jnp.broadcast_to(row.astype(F32), (TAIL, row.shape[1]))
    first = lax.broadcasted_iota(jnp.int32, wide.shape, 0) == 0
    return jnp.where(first, wide, 0.0)


def mass_of(tail, quarter):
    row = tail[0:1, :].astype(F32)
    return row[:, :quarter] + row[:, quarter : 2 * quarter] + row[:, 2 * quarter : 3 * quarter]


def packet_tail(weights, centroids):
    quarter, width = centroids.shape
    rows = []
    for k in range(quarter // TILE):
        base = centroids[k * TILE : (k + 1) * TILE].astype(F32)
        rows.append(to_row(jnp.sum(base * base, axis=1, keepdims=True)))
    offsets = weights - jnp.concatenate(rows, axis=1) * (16.0 / width)
    terms = split_masses(offsets).astype(F32)
    line = lax.broadcasted_iota(jnp.int32, (TAIL, quarter), 0)
    spread = jnp.zeros((TAIL, quarter), F32)
    for k in range(3):
        spread = jnp.where(line == k, terms[:, k * quarter : (k + 1) * quarter], spread)
    first = jnp.where(line == 0, weights, 0.0)
    rest = jnp.zeros((TAIL, width - 2 * quarter), F32)
    return jnp.concatenate([first, spread, rest], axis=1).astype(BF16)


def mass_row(macc, start, quarter):
    ones = jnp.ones((8, TILE), F32)
    rows = [
        lax.dot_general(
            ones,
            macc[pl.ds(start + k * TILE, TILE), :],
            (((1,), (1,)), ((), ())),
            precision=lax.Precision.HIGHEST,
            preferred_element_type=F32,
        )[0:1]
        for k in range(quarter // TILE)
    ]
    return jnp.concatenate(rows, axis=1)


def hand_over(core, rows, sides, acc, macc, sends, keeps):
    quarter = rows // 4
    packet = quarter + TAIL
    half = rows // 2
    for side in range(sides):
        for y in range(2):
            mine = pl.multiple_of(side * rows + core * half + y * quarter, quarter)
            other = pl.multiple_of(side * rows + (1 - core) * half + y * quarter, quarter)
            body = pl.ds(y * packet, quarter)
            tail = pl.ds(y * packet + quarter, TAIL)
            sends[side][body, :] = acc[pl.ds(other, quarter), :].astype(BF16)
            sends[side][tail, :] = tail_of(split_masses(mass_row(macc, other, quarter))).astype(
                BF16
            )
            row = mass_row(macc, mine, quarter)
            keeps[side][body, :] = acc[pl.ds(mine, quarter), :]
            keeps[side][tail, :] = tail_of(jnp.concatenate([row, row * 0.0, row * 0.0], axis=1))


def clear(acc, macc):
    @pl.loop(0, acc.shape[0] // BLOCK)
    def _(b):
        at = pl.ds(pl.multiple_of(b * BLOCK, BLOCK), BLOCK)
        acc[at, :] = jnp.zeros((BLOCK, acc.shape[1]), F32)
        macc[at, :] = jnp.zeros((BLOCK, TILE), F32)


def tiles_kernel(rows, sizes, ids_ref, me_ref, points_ref, *refs):
    quarter = rows // 4
    count = sum(len(parts) for side in sizes for parts in side)
    parts_refs = list(refs[:count])
    sends = refs[count : count + 3]
    keeps = refs[count + 3 : count + 6]
    near, tails, offs, acc, macc, held, in_sem, held_sem = refs[count + 6 :]
    step = pl.program_id(0)
    core = me_ref[0]
    plane = me_ref[1]

    def arrivals():
        out = []
        left = list(parts_refs)
        for side in range(3):
            for j in range(4):
                c = core if j < 2 else 1 - core
                y = plane if j % 2 == 0 else 1 - plane
                at = side * 4 + c * 2 + y
                first = 0
                for size in sizes[side][j]:
                    ref = left.pop(0)
                    last = min(first + size, quarter)
                    out.append(
                        pltpu.make_async_copy(
                            ref.at[pl.ds(0, last - first)],
                            near.at[
                                pl.ds(pl.multiple_of(at * quarter + first, TILE // 2), last - first)
                            ],
                            in_sem.at[len(out)],
                        )
                    )
                    if first + size > quarter:
                        out.append(
                            pltpu.make_async_copy(
                                ref.at[pl.ds(last - first, TAIL)],
                                tails.at[pl.ds(pl.multiple_of(at * TAIL, TAIL), TAIL)],
                                in_sem.at[len(out)],
                            )
                        )
                    first = last
        return out

    width = near.shape[1]
    step_rows = STEP_TILES * TILE

    def points_copy(n):
        at = pl.ds(pl.multiple_of(n * step_rows, step_rows), step_rows)
        return pltpu.make_async_copy(points_ref.at[at], held.at[at], held_sem.at[n])

    def rows_at(t):
        return pl.ds(pl.multiple_of(step * step_rows + t * TILE, TILE), TILE)

    @pl.when(step == 0)
    def _():
        copies = arrivals()
        for copy in copies:
            copy.start()
        for n in range(held.shape[0] // step_rows):
            points_copy(n).start()
        clear(acc, macc)
        for copy in copies:
            copy.wait()
        ones = jnp.ones((TAIL, TILE), BF16)
        for n in range(12):
            for k in range(quarter // TILE):
                terms = tails[n * TAIL : (n + 1) * TAIL, quarter + k * TILE : quarter + (k + 1) * TILE]
                offs[pl.ds(n * quarter + k * TILE, TILE), :] = lax.dot_general(
                    terms, ones, (((0,), (0,)), ((), ())), preferred_element_type=F32
                )

    def blocks_of(t, slots):
        tile = step * STEP_TILES + t
        return [
            pl.ds(pl.multiple_of(ids_ref[tile * SLOTS + k] * BLOCK, BLOCK), BLOCK) for k in slots
        ]

    points_copy(step).wait()
    members = []
    for t in range(STEP_TILES):
        points = held[rows_at(t), :]
        at = blocks_of(t, (0, 2, 1, 3))
        cand = jnp.concatenate([near[a, :] for a in at], axis=0)
        off = jnp.concatenate([offs[a, :] for a in at], axis=0)
        scores = lax.dot_general(
            cand, points, (((1,), (1,)), ((), ())), preferred_element_type=F32
        )
        scores = scores * (32.0 / width) + off
        top = jnp.max(scores, axis=0, keepdims=True)
        raw = jnp.exp(scores - top)
        total = jnp.sum(raw, axis=0, keepdims=True)
        member = (raw * (1.0 / total)).astype(BF16)
        members.append(member)
    for t in range(STEP_TILES):
        points = held[rows_at(t), :]
        at = blocks_of(t, (0, 2, 1, 3))
        numerator = jnp.dot(members[t], points, preferred_element_type=F32)
        masses = members[t].astype(F32)
        for k in range(SLOTS):
            acc[at[k], :] += numerator[k * BLOCK : (k + 1) * BLOCK]
            macc[at[k], :] += masses[k * BLOCK : (k + 1) * BLOCK]

    @pl.when(step == pl.num_programs(0) - 1)
    def _():
        hand_over(core, rows, 3, acc, macc, sends, keeps)


def assign_tiles(points, ids, me, packets, rows):
    count, width = points.shape
    quarter = rows // 4
    packet = quarter + TAIL
    tiles = count // TILE
    any_spec = pl.BlockSpec(memory_space=pl.ANY)
    vmem_spec = pl.BlockSpec(memory_space=pltpu.VMEM)
    step_rows = STEP_TILES * TILE
    sizes = [[[part.shape[0] for part in parts] for parts in side] for side in packets]
    arrays = [part for side in packets for parts in side for part in parts]
    outs = pl.pallas_call(
        functools.partial(tiles_kernel, rows, sizes),
        grid_spec=pltpu.PrefetchScalarGridSpec(
            num_scalar_prefetch=2,
            grid=(tiles // STEP_TILES,),
            in_specs=[pl.BlockSpec(memory_space=pltpu.HBM)] + [any_spec] * len(arrays),
            out_specs=[vmem_spec] * 6,
            scratch_shapes=[
                pltpu.VMEM((3 * rows, width), BF16),
                pltpu.VMEM((12 * TAIL, width), BF16),
                pltpu.VMEM((3 * rows, TILE), F32),
                pltpu.VMEM((3 * rows, width), F32),
                pltpu.VMEM((3 * rows, TILE), F32),
                pltpu.VMEM((count, width), BF16),
                pltpu.SemaphoreType.DMA((len(arrays) + 12,)),
                pltpu.SemaphoreType.DMA((tiles // STEP_TILES,)),
            ],
        ),
        out_shape=[jax.ShapeDtypeStruct((2 * packet, width), BF16)] * 3
        + [jax.ShapeDtypeStruct((2 * packet, width), F32)] * 3,
        compiler_params=pltpu.CompilerParams(vmem_limit_bytes=VMEM_LIMIT),
        cost_estimate=pl.CostEstimate(
            flops=4 * count * SLOTS * BLOCK * width,
            bytes_accessed=2 * count * width,
            transcendentals=count * SLOTS * BLOCK,
        ),
        name="tiles",
    )(ids, me, points, *arrays)
    return outs[:3], outs[3:]


def small_call(kernel, me, arrays, outs, name, after=()):
    vmem_spec = pl.BlockSpec(memory_space=pltpu.VMEM)
    return pl.pallas_call(
        kernel,
        in_specs=[pl.BlockSpec(memory_space=pltpu.SMEM)]
        + [vmem_spec] * len(arrays)
        + [pl.BlockSpec(memory_space=pl.ANY)] * len(after),
        out_specs=[vmem_spec] * len(outs),
        out_shape=outs,
        compiler_params=pltpu.CompilerParams(vmem_limit_bytes=SMALL_LIMIT),
        cost_estimate=pl.CostEstimate(
            flops=sum(a.size for a in arrays),
            bytes_accessed=sum(a.size * a.dtype.itemsize for a in arrays),
            transcendentals=0,
        ),
        name=name,
    )(me, *arrays, *after)


def sum_kernel(quarter, pairs, singles, base, outputs, me_ref, *refs):
    terms = refs[: pairs + singles]
    outs = refs[len(refs) - len(outputs) :]

    def rows_of(start, first, size):
        at = [pl.ds(pl.multiple_of(start + first, TAIL), size)] * pairs
        at += [pl.ds(first - base, size)] * singles
        return [term[a, :] for term, a in zip(terms, at)]

    for (over, first, last), out in zip(outputs, outs):
        start = (1 - me_ref[1] if over else me_ref[1]) * (quarter + TAIL)
        size = last - first
        body = rows_of(start, first, size)
        out[pl.ds(0, size), :] = sum(r.astype(F32) for r in body).astype(BF16)
        if last == quarter:
            mass = sum(mass_of(r, quarter) for r in rows_of(start, quarter, TAIL))
            out[pl.ds(size, TAIL), :] = tail_of(split_masses(mass)).astype(BF16)


def add_packets(me, pairs, singles, outputs, base=0, after=()):
    packet, width = pairs[0].shape[0] // 2, pairs[0].shape[1]
    quarter = packet - TAIL
    return small_call(
        functools.partial(sum_kernel, quarter, len(pairs), len(singles), base, outputs),
        me,
        [*pairs, *singles],
        [jax.ShapeDtypeStruct((part_rows(p[1:], quarter), width), BF16) for p in outputs],
        "add_packets",
        after,
    )


def renew_kernel(quarter, target, ranges_in, ranges_out, me_ref, base, keep, beside, *refs):
    terms = list(zip(ranges_in, refs))
    outs = list(zip(ranges_out, refs[len(terms) :]))
    start = me_ref[1] * (quarter + TAIL)
    mass = sum(
        mass_of(ref[pl.ds(last - first, TAIL), :], quarter)
        for (first, last), ref in terms
        if last == quarter
    )
    for term in (keep, beside):
        tail = term[pl.ds(pl.multiple_of(start + quarter, TAIL), TAIL), :]
        mass = mass + mass_of(tail, quarter)
    weights = base[pl.ds(quarter, TAIL), :].astype(F32)[0:1, :quarter]
    renewed = weights + dual_step * (1.0 - mass / target)
    renewed = renewed.astype(BF16).astype(F32)
    blocks = []
    for row in range(0, quarter, TILE):
        here = pl.ds(pl.multiple_of(start + row, TAIL), TILE)
        total = keep[here, :] + beside[here, :].astype(F32)
        for (first, last), ref in terms:
            if first <= row < last:
                total = total + ref[pl.ds(row - first, TILE), :].astype(F32)
        column = to_column(mass[:, row : row + TILE]) + prior_mass
        total = total + prior_mass * base[pl.ds(row, TILE), :].astype(F32)
        blocks.append((total / column).astype(BF16))
    tail = packet_tail(renewed, jnp.concatenate(blocks, axis=0))
    for (first, last), out in outs:
        for row in range(first, last, TILE):
            out[pl.ds(row - first, TILE), :] = blocks[row // TILE]
        if last == quarter:
            out[pl.ds(last - first, TAIL), :] = tail


def renew(me, base, pair, terms, ranges_in, target, ranges_out):
    packet, width = base.shape
    quarter = packet - TAIL
    return small_call(
        functools.partial(renew_kernel, quarter, target, ranges_in, ranges_out),
        me,
        [base, *pair, *terms],
        [jax.ShapeDtypeStruct((part_rows(p, quarter), width), BF16) for p in ranges_out],
        "renew",
    )


def start_kernel(quarter, which, me_ref, centroids, weights, *refs):
    outs = refs[: len(which)]
    block, sem = refs[len(which) :]
    core, plane = me_ref[0], me_ref[1]
    places = []
    for c, y, first, last in which:
        if (c, y) not in places:
            places.append((c, y))
    copies = []
    for n, (c, y) in enumerate(places):
        place = (core if c else 1 - core) * 2 + (plane if y else 1 - plane)
        at = pl.multiple_of(place * quarter, quarter)
        copies.append(
            pltpu.make_async_copy(centroids.at[pl.ds(at, quarter)], block.at[n], sem.at[n])
        )
        copies[-1].start()
    for n, (c, y) in enumerate(places):
        place = (core if c else 1 - core) * 2 + (plane if y else 1 - plane)
        lines = jnp.zeros((1, quarter), F32)
        for q in range(4):
            lines = jnp.where(place == q, weights[q : q + 1, :].astype(F32), lines)
        copies[n].wait()
        rows = block[n]
        tail = packet_tail(lines, rows)
        for (oc, oy, first, last), out in zip(which, outs):
            if (oc, oy) == (c, y):
                out[pl.ds(0, last - first), :] = rows[first:last]
                if last == quarter:
                    out[pl.ds(last - first, TAIL), :] = tail


def start_packets(me, centroids, weights, which):
    rows, width = centroids.shape
    quarter = rows // 4
    vmem_spec = pl.BlockSpec(memory_space=pltpu.VMEM)
    return pl.pallas_call(
        functools.partial(start_kernel, quarter, which),
        in_specs=[
            pl.BlockSpec(memory_space=pltpu.SMEM),
            pl.BlockSpec(memory_space=pltpu.HBM),
            vmem_spec,
        ],
        out_specs=[vmem_spec] * len(which),
        out_shape=[
            jax.ShapeDtypeStruct((part_rows(p[2:], quarter), width), BF16) for p in which
        ],
        scratch_shapes=[pltpu.VMEM((3, quarter, width), BF16), pltpu.SemaphoreType.DMA((3,))],
        compiler_params=pltpu.CompilerParams(vmem_limit_bytes=SMALL_LIMIT),
        name="start_packets",
    )(me, centroids, weights)


def finish_kernel(rows, parts, me_ref, *refs):
    quarter = rows // 4
    n = 4 * len(parts)
    packets = refs[:n]
    out, weights_out, tails, sem = refs[n:]
    core, plane = me_ref[0], me_ref[1]
    copies = []
    places = []
    for j in range(4):
        c = core if j < 2 else 1 - core
        y = plane if j % 2 == 0 else 1 - plane
        places.append(c * 2 + y)
        for k, (first, last) in enumerate(parts):
            ref = packets[j * len(parts) + k]
            at = pl.multiple_of(places[j] * quarter + first, TILE)
            copies.append(
                pltpu.make_async_copy(
                    ref.at[pl.ds(0, last - first)],
                    out.at[pl.ds(at, last - first)],
                    sem.at[len(copies)],
                )
            )
            if last == quarter:
                copies.append(
                    pltpu.make_async_copy(
                        ref.at[pl.ds(last - first, TAIL)], tails.at[j], sem.at[len(copies)]
                    )
                )
    for copy in copies:
        copy.start()
    for copy in copies:
        copy.wait()
    found = [tails[j][0:1, :quarter].astype(F32) for j in range(4)]
    lines = []
    for q in range(4):
        line = found[0]
        for j in range(1, 4):
            line = jnp.where(places[j] == q, found[j], line)
        lines.append(line)
    weights_out[...] = jnp.concatenate(lines, axis=0).astype(BF16)


def finish(me, own, rows):
    width = own[0][0].shape[1]
    quarter = rows // 4
    parts = ranges(quarter)
    arrays = [part for packet in own for part in packet]
    any_spec = pl.BlockSpec(memory_space=pl.ANY)
    return pl.pallas_call(
        functools.partial(finish_kernel, rows, parts),
        in_specs=[pl.BlockSpec(memory_space=pltpu.SMEM)] + [any_spec] * len(arrays),
        out_specs=[any_spec, pl.BlockSpec(memory_space=pltpu.VMEM)],
        out_shape=[
            jax.ShapeDtypeStruct((rows, width), BF16),
            jax.ShapeDtypeStruct((4, quarter), BF16),
        ],
        scratch_shapes=[
            pltpu.VMEM((4, TAIL, width), BF16),
            pltpu.SemaphoreType.DMA((len(arrays) + 4,)),
        ],
        compiler_params=pltpu.CompilerParams(vmem_limit_bytes=SMALL_LIMIT),
        name="finish",
    )(me, *arrays)


def per_device(points, block_lists, centroids, dual_weights):
    rows, width = centroids.shape
    quarter = rows // 4
    own_blocks = rows // BLOCK
    position = lax.axis_index("blk")
    groups = lax.axis_size("group")
    member = lax.axis_index("group")
    core, plane = member % 2, member // 2
    me = jnp.stack([core, plane]).astype(jnp.int32)
    target = points.shape[0] * groups / rows
    parts = ranges(quarter)
    owner = block_lists // own_blocks
    side = jnp.where(owner == position, 2, jnp.where(owner == position ^ 1, 1, 0))
    near_ids = side * own_blocks + block_lists % own_blocks
    near_ids = near_ids.reshape(-1).astype(jnp.int32)

    def each(move, arrays):
        return [move(a) for a in arrays]

    lines = dual_weights.reshape(4, quarter)
    everything = (0, quarter)
    low, high = parts
    [mine] = start_packets(me, centroids, lines, [(1, 1, *everything)])
    for sweep in range(ITERS):
        far, near = cross_swap(mine), pair_swap(mine)
        if sweep == 0:
            which = [(c, y, *everything) for c, y in ((1, 0), (0, 1), (0, 0))]
            own = [mine, *start_packets(me, centroids, lines, which)]
            beside = own[1]
        else:
            beside = plane_swap(mine)
            own = [mine, beside, core_swap(mine), core_swap(beside)]
        near_beside = pair_swap(beside)
        far_beside = plane_swap(far)
        packets = [
            [far, far_beside, core_swap(far), core_swap(far_beside)],
            [near, near_beside, core_swap(near), core_swap(near_beside)],
            own,
        ]
        packets = [[[packet] for packet in side] for side in packets]
        sends, keeps = assign_tiles(points, near_ids, me, packets, rows)
        far_pair, near_pair, own_pair = [(k, core_swap(a)) for a, k in zip(sends, keeps)]
        far_sums = add_packets(me, far_pair, [], [(True, *high), (True, *low)])
        far_over_high, far_over_low = each(plane_swap, far_sums)
        near_sums = add_packets(
            me, near_pair, [], [(True, *low), (True, *high), (False, *low)]
        )
        near_over_low, near_over_high, near_here_low = each(pair_swap, near_sums)
        [far_high] = add_packets(
            me, far_pair, [far_over_high], [(False, *high)], high[0], [near_over_low]
        )
        far_high = inward(far_high)
        [far_low] = add_packets(
            me, far_pair, [far_over_low], [(False, *low)], low[0], [near_over_high]
        )
        far_here_low = cross_swap(far_low)
        own_low = add_packets(me, own_pair, [near_over_low], [(True, *low)], low[0])
        own_high = add_packets(me, own_pair, [near_over_high], [(True, *high)], high[0])
        own_over_low, own_over_high = each(plane_swap, [*own_low, *own_high])
        [near_high] = add_packets(
            me,
            near_pair,
            [far_high],
            [(False, *high)],
            high[0],
            [near_here_low, *own_low, *own_high],
        )
        near_here_high = pair_swap(near_high)
        last = sweep == ITERS - 1
        mine_parts = renew(
            me,
            mine,
            own_pair,
            [own_over_low, own_over_high, near_here_low, near_here_high, far_here_low],
            [low, high, low, high, low],
            target,
            parts if last else [everything],
        )
        mine = mine_parts[0]
    beside = each(plane_swap, mine_parts)
    own = [mine_parts, beside, each(core_swap, mine_parts), each(core_swap, beside)]
    new_centroids, new_weights = finish(me, own, rows)
    return (new_centroids, new_weights.reshape(rows))


def solution(mesh):
    return jax.shard_map(
        per_device,
        mesh=mesh,
        in_specs=(P(("group", "blk"), None), P(("group", "blk"), None), P("blk", None), P("blk")),
        out_specs=(P("blk", None), P("blk")),
        check_vma=False,
    )
```
